32 devices in a mesh: strip: 2 (over x), sub: 16 (over z, y, core).
Axes of the slice: x: 2, y: 2, z: 4, core: 2. Of those that a mesh axis runs over, the one named last changes fastest.
Arguments:
- images: float32 [2, 64, 262144], P(None, None, ('strip', 'sub')), parts along dimension 2, may hold values from -6 to 6
- band_shift: int32 [32, 2, 2, 64, 64], P(('strip', 'sub')), parts along dimension 0, may hold values from 0 to 3
- tap_weights: float32 [32, 2, 2, 64, 4], P(('strip', 'sub')), parts along dimension 0, may hold values from -3 to 3
- phases: float32 [32, 2, 2, 64, 2], P(('strip', 'sub')), parts along dimension 0, may hold values from -3.140625 to 3.140625
- extent_map: int32 [32], P('strip'), parts along dimension 0, may hold values from 16 to 48, as said below
Outputs:
- packed: float32 [2, 64, 131072], P(None, None, ('strip', 'sub')), parts along dimension 2
The draws below stay inside these ranges and needn't reach their ends.
There are 2 independent parts, one for each index of `strip`. The reference program is written for one: setup_inputs(seed, part) draws one part's arguments, and reference() takes and returns one part's arrays. A program takes and returns all parts, laid end to end along the dimension named above; each array names one. Nothing has to cross between parts.
Inputs may be any that keep to these rules, and one draw needn't show every extreme that they name: For every k, extent_map[2k] + extent_map[2k + 1] = 64.
All inputs are finite; a program needn't handle non-finite values.
Results may differ from the reference program's by a relative error of at most 0.0003.
Values sent between devices are 32-bit elements; how exact they have to be, the bound alone decides.
No kernel may reach another device: no remote copies, remote signals or barrier semaphores. Data moves between devices by JAX's collectives and lax.ppermute only.
A program may use at most 128 MiB of HBM per device.

```python
from functools import partial
import jax
import jax.numpy as jnp

BEAMS = 64
ROWS = 8192
BLK = 128
NBLK = 64
SLOTS = 32
CHILD_ROWS = 131072
N_SUB = 16


def draw_extent_map(key, part):
    key = jax.random.fold_in(key, 7)
    pair_count = N_SUB // 2
    first_key, second_key = jax.random.split(key)
    even_part = jax.random.randint(first_key, (pair_count,), SLOTS // 2, 3 * SLOTS // 2 + 1)
    order_list = jax.random.permutation(second_key, pair_count)
    even_part = even_part.at[order_list[0]].set(3 * SLOTS // 2)
    even_part = even_part.at[order_list[1]].set(SLOTS // 2)
    return jnp.stack([even_part, 2 * SLOTS - even_part], axis=1).reshape(N_SUB).astype(jnp.int32)


def set_ends(entries, own_key, low, high):
    extent = entries.shape
    index_at = [jax.random.randint(jax.random.fold_in(own_key, axis), (), 0, extent[axis]) for axis in range(len(extent))]
    entries = entries.at[tuple(index_at)].set(low)
    longest = extent.index(max(extent))
    index_at[longest] = (index_at[longest] + 1) % extent[longest]
    return entries.at[tuple(index_at)].set(high)


def levels(key, dims, shards, low, top_value):
    loudness = 1.0
    for position, parts in shards:
        heights = jax.random.uniform(jax.random.fold_in(jax.random.fold_in(key, 6), position), (parts,), jnp.float32, low / len(shards), top_value / len(shards))
        loudness = loudness * jnp.repeat(jnp.exp(heights), dims[position] // parts).reshape((-1,) + (1,) * (len(dims) - 1 - position))
    return loudness


def scatter_about(rng, dims, width, reach, pieces=(), kind=jnp.bfloat16):
    factor_of = levels(rng, dims, pieces, -0.22, 0.18) if pieces else 1.0
    values = jax.random.normal(rng, dims, jnp.float32) * width * factor_of
    return jnp.minimum(jnp.maximum(values, -reach), reach).astype(kind)


def setup_inputs(seed: int = 0, part: int = 0) -> dict:
    splits = jax.random.split(jax.random.key(seed), 6)
    part_splits = jax.random.split(jax.random.fold_in(splits[5], part), 6)
    return {
        "images": scatter_about(part_splits[0], (2, BEAMS, CHILD_ROWS), 1.0, 6.0, ((2, 16),), jnp.float32),
        "band_shift": set_ends(jax.random.randint(part_splits[1], (N_SUB, 2, 2, BEAMS, NBLK), 0, 4), jax.random.fold_in(part_splits[1], 1), 0, 3).astype(jnp.int32),
        "tap_weights": scatter_about(part_splits[2], (N_SUB, 2, 2, BEAMS, 4), 0.5, 3.0, ((0, 16),), jnp.float32),
        "phases": jnp.clip(jax.random.uniform(part_splits[3], (N_SUB, 2, 2, BEAMS, 2), jnp.float32, -3.140625, 3.140625), -3.140625, 3.140625),
        "extent_map": draw_extent_map(jax.random.fold_in(jax.random.fold_in(splits[5], part), 71), part),
    }


def merge_level(sources, band_shift, tap_weights, phases, out_rows, total_rows, block_rows):
    widened = jnp.repeat(sources, 2, axis=2)
    rows_in = widened.shape[3]
    right = max(0, out_rows + 5 - rows_in)
    padded = jnp.pad(widened, ((0, 0), (0, 0), (0, 0), (1, right)))
    shifts = jnp.repeat(band_shift[:, :, : out_rows // block_rows], block_rows, axis=2)
    summed = jnp.zeros(widened.shape[:3] + (out_rows,), jnp.float32)
    for offset in range(-1, 6):
        weight = jnp.zeros(shifts.shape, jnp.float32)
        for tap_index in range(4):
            weight = weight + jnp.where(shifts == offset + 1 - tap_index, tap_weights[:, :, tap_index:tap_index + 1], 0.0)
        summed = summed + weight[:, None] * padded[:, :, :, 1 + offset:1 + offset + out_rows]
    row_phase = jnp.arange(out_rows).astype(jnp.float32) / total_rows
    angle = phases[:, :, 0:1] + phases[:, :, 1:2] * row_phase
    cosine = jnp.cos(angle)
    sine_part = jnp.sin(angle)
    real_part = cosine * summed[:, 0] - sine_part * summed[:, 1]
    imag_part = sine_part * summed[:, 0] + cosine * summed[:, 1]
    return jnp.stack([real_part[0] + real_part[1], imag_part[0] + imag_part[1]])


def pick_halves(fields, bit):
    count = fields.shape[0]
    half_beams = fields.shape[2] // 2
    index_all = jnp.arange(count)
    side = (index_all >> bit) & 1
    first_source = index_all - side * (1 << bit)
    lower = fields[:, :, :half_beams]
    higher = fields[:, :, half_beams:]
    pick_side = (side == 0)[:, None, None, None]

    def take_from(source):
        return jnp.where(pick_side, lower[source], higher[source])

    return jnp.stack([take_from(first_source), take_from(first_source + (1 << bit))], axis=1)


def reference(images, band_shift, tap_weights, phases, extent_map):
    count = N_SUB
    top_bit = N_SUB.bit_length() - 2
    children = images.reshape(2, BEAMS, count, ROWS).transpose(2, 0, 1, 3)
    merger = jax.vmap(partial(merge_level, out_rows=ROWS, total_rows=ROWS, block_rows=BLK))
    first_level = merger(pick_halves(children, 0), band_shift[:, 0], tap_weights[:, 0], phases[:, 0])
    second_level = merger(pick_halves(first_level, top_bit), band_shift[:, 1], tap_weights[:, 1], phases[:, 1])
    blocks = second_level.reshape(count, 2, BEAMS, NBLK, BLK)
    pair_count = count // 2
    slot_ids = jnp.arange(2 * SLOTS)
    even_extent = extent_map[0::2][:, None]
    from_even = slot_ids[None, :] < even_extent
    device_pick = jnp.arange(pair_count)[:, None] * 2 + jnp.where(from_even, 0, 1)
    block_pick = jnp.where(from_even, slot_ids[None, :], slot_ids[None, :] - even_extent)
    gathered = blocks[device_pick, :, :, block_pick]
    gathered = gathered.reshape(count * SLOTS, 2, BEAMS, BLK).transpose(1, 2, 0, 3)
    return gathered.reshape(2, BEAMS, count * SLOTS * BLK)
```

```python
import functools

import jax
import jax.numpy as jnp
from jax import lax
from jax.experimental import pallas as pl
from jax.experimental.pallas import tpu as pltpu
from jax.sharding import PartitionSpec as P

BLK = 128
ROW = 32
QRT = 16
CHUNKS = (14, 10, 8)


class Sizes:
    def __init__(self, slots, total_rows):
        self.slots = slots
        self.total = total_rows
        self.right = slots + 1
        self.middle = slots + 2
        self.zero = slots + 3
        self.used = slots + 3
        self.cols = 3 * slots // 2 + 1


ANY = pl.BlockSpec(memory_space=pl.ANY)
SMEM = pl.BlockSpec(memory_space=pltpu.SMEM)
F32 = jnp.float32


def shape(*dims):
    return jax.ShapeDtypeStruct(dims, F32)


def call(body, ins, outs, scratch, flops, aliases=None):
    size = sum(4 * x.size for x in ins) + sum(4 * x.size for x in outs)
    return pl.pallas_call(
        body,
        out_shape=tuple(outs),
        in_specs=[SMEM] + [ANY] * (len(ins) - 1),
        out_specs=tuple([ANY] * len(outs)),
        scratch_shapes=scratch,
        input_output_aliases=aliases or {},
        compiler_params=pltpu.CompilerParams(vmem_limit_bytes=48 * 2**20),
        cost_estimate=pl.CostEstimate(flops=flops, bytes_accessed=size, transcendentals=0),
    )(*ins)


def place(extent_ref):
    pos = lax.axis_index("sub")
    top = lax.axis_size("sub").bit_length() - 2
    core = pos & 1
    side = (pos >> top) & 1
    even = pos - core
    return core, side, extent_ref[even], extent_ref[even ^ (1 << top)]


def copy_block(images_ref, dst, side, part, block, sem):
    rows = pl.ds(pl.multiple_of(part * 2 * QRT + side * QRT, QRT), QRT)
    lanes = pl.ds(pl.multiple_of(block * BLK, BLK), BLK)
    pltpu.make_async_copy(images_ref.at[:, rows, lanes], dst, sem).start()


def copy_slots(images_ref, dst_ref, base, side, extent, first, count, sem):
    def step(i, carry):
        slot = first + i
        part = (slot >= extent).astype(jnp.int32)
        copy_block(images_ref, dst_ref.at[base + i], side, part, slot - part * extent, sem)
        return carry

    lax.fori_loop(0, count, step, 0)


def copy_halo(images_ref, dst_ref, left_at, right_at, middle_at, side, extent, first, slots, sem):
    part = (first >= extent).astype(jnp.int32)
    block = jnp.maximum(first - part * extent - 1, 0)
    copy_block(images_ref, dst_ref.at[left_at], side, part, block, sem)
    last = first + slots - 1
    part = (last >= extent).astype(jnp.int32)
    copy_block(images_ref, dst_ref.at[right_at], side, part, last - part * extent + 1, sem)
    copy_block(images_ref, dst_ref.at[middle_at], side, 0, extent, sem)


def wait_whole(ref, sem):
    pltpu.make_async_copy(ref, ref, sem).wait()


def first_pack(sz, extent_ref, images_ref, same_ref, cross_ref, sems):
    core, side, _, extent = place(extent_ref)
    count = same_ref.shape[0]
    copy_slots(images_ref, same_ref, 0, 1 - side, extent, core * sz.slots, count, sems.at[0])
    copy_slots(images_ref, cross_ref, 0, 1 - side, extent, (1 - core) * sz.slots, count, sems.at[1])
    wait_whole(same_ref, sems.at[0])
    wait_whole(cross_ref, sems.at[1])


def rest_pack(sz, chunks, extent_ref, images_ref, par0_ref, par1_ref, *rest):
    outs, sems = rest[:-1], rest[-1]
    halo_same, halo_cross, mate, kept = outs[:4]
    core, side, own, other = place(extent_ref)
    slots = sz.slots
    n = 0
    for ref, window in ((halo_same, core), (halo_cross, 1 - core)):
        copy_halo(images_ref, ref, 0, 1, 2, 1 - side, other, window * slots, slots, sems.at[n])
        pltpu.make_async_copy(par0_ref.at[1 - side], ref.at[3], sems.at[n]).start()
        n += 1
    begin = chunks[0]
    for k, count in enumerate(chunks[1:]):
        for ref, window in ((outs[4 + 2 * k], core), (outs[5 + 2 * k], 1 - core)):
            copy_slots(images_ref, ref, 0, 1 - side, other, window * slots + begin, count, sems.at[n + 2])
            n += 1
        begin += count
    for at, ref, window in ((2, mate, 1 - core), (3, kept, core)):
        copy_slots(images_ref, ref, 1, side, own, window * slots, slots, sems.at[at])
        copy_halo(images_ref, ref, 0, sz.right, sz.middle, side, own, window * slots, slots, sems.at[at])
    pltpu.make_async_copy(par0_ref.at[side], mate.at[sz.used], sems.at[2]).start()
    pltpu.make_async_copy(par1_ref.at[0], mate.at[sz.used + 1], sems.at[2]).start()
    pltpu.make_async_copy(par1_ref.at[1], mate.at[sz.used + 2], sems.at[2]).start()
    for i, ref in enumerate(outs):
        wait_whole(ref, sems.at[i])


def build_tables(sz, par_ref, tab_ref, ltab_ref, groups, extent, first):
    lane = lax.broadcasted_iota(jnp.int32, (QRT, BLK), 1)
    even = first + lane - 1 < extent
    middle = lane == sz.middle
    even = jnp.logical_or(even, middle)
    block = jnp.where(even, first - 1 + lane, first - 1 + lane - extent)
    block = jnp.where(middle, extent, block).astype(F32)
    for group in range(groups):
        rows = [par_ref[p, pl.ds(group, QRT, stride=groups), :] for p in range(2)]
        for s in range(2):
            off = s * (BLK // 2)

            def column(c):
                return jnp.where(
                    even,
                    jnp.broadcast_to(rows[0][:, off + c : off + c + 1], (QRT, BLK)),
                    jnp.broadcast_to(rows[1][:, off + c : off + c + 1], (QRT, BLK)),
                )

            turn = lambda x, by: pltpu.roll(x, jnp.bitwise_and(by, BLK - 1), 1)
            shift = jnp.where(
                even, turn(rows[0], 1 - first - off), turn(rows[1], 1 - first + extent - off)
            )
            shift = jnp.where(middle, turn(rows[0], sz.middle - extent - off), shift)
            taps = [column(sz.cols + k) for k in range(4)]
            for o in range(-1, 6):
                weight = jnp.zeros((QRT, BLK), F32)
                for k in range(4):
                    if 0 <= o + 1 - k <= 3:
                        weight = weight + jnp.where(shift == float(o + 1 - k), taps[k], 0.0)
                tab_ref[s, group, o + 1] = weight
            angle = column(sz.cols + 4) + column(sz.cols + 5) * (block * (BLK / sz.total))
            tab_ref[s, group, 7] = jnp.cos(angle)
            tab_ref[s, group, 8] = jnp.sin(angle)
            for p in range(2):
                c = off + sz.cols + 5
                angle = jnp.broadcast_to(rows[p][:, c : c + 1], (QRT, BLK)) * (
                    lane.astype(F32) / sz.total
                )
                ltab_ref[p, s, group, 0] = jnp.cos(angle)
                ltab_ref[p, s, group, 1] = jnp.sin(angle)


def merge_block(load, tab_ref, ltab_ref, groups, x, before, after, part, h, store):
    lane = lax.broadcasted_iota(jnp.int32, (8, BLK), 1)
    pick = jnp.full((8, BLK), x, jnp.int32)
    rows = pl.ds(8 * h, 8)
    sums = [[None, None], [None, None]]
    for s in range(2):
        moved = []
        for ri in range(2):
            cur, prv, nxt = load(s, x, ri), load(s, before, ri), load(s, after, ri)
            views = [pltpu.roll(jnp.where(lane == BLK - 1, prv, cur), 1, 1), cur]
            for o in range(1, 6):
                views.append(pltpu.roll(jnp.where(lane < o, nxt, cur), BLK - o, 1))
            moved.append(views)
        for u in range(2):
            spread = [
                jnp.take_along_axis(tab_ref[s, groups[u], k, rows, :], pick, axis=1) for k in range(9)
            ]
            value = []
            for ri in range(2):
                total = spread[0] * moved[ri][0]
                for k in range(1, 7):
                    total = total + spread[k] * moved[ri][k]
                value.append(total)
            cl = ltab_ref[part, s, groups[u], 0, rows, :]
            sl = ltab_ref[part, s, groups[u], 1, rows, :]
            cosine = spread[7] * cl - spread[8] * sl
            sine = spread[8] * cl + spread[7] * sl
            real = cosine * value[0] - sine * value[1]
            imag = sine * value[0] + cosine * value[1]
            sums[u] = [real, imag] if s == 0 else [sums[u][0] + real, sums[u][1] + imag]
    for u in range(2):
        for ri in range(2):
            store(u, ri, sums[u][ri])


def level_one(sz, d_ref, f_ref, tab_ref, ltab_ref, x, before, after, part):
    for h in range(2):
        rows = lambda ri: pl.ds(QRT * ri + 8 * h, 8)

        def store(u, ri, value):
            f_ref[x, u, rows(ri), :] = value

        merge_block(
            lambda s, at, ri: d_ref[s, at, rows(ri), :],
            tab_ref, ltab_ref, (0, 1), x, before, after, part, h, store,
        )


def level_two(sz, f_ref, out_ref, at, tab_ref, ltab_ref, x, before, after, part):
    for u1 in range(2):
        for h in range(2):
            rows = pl.ds(8 * h, 8)

            def store(u, ri, value):
                out_ref[at, ri, pl.ds(32 * h + 2 * u1 + u, 8, stride=4), :] = value

            merge_block(
                lambda s, pos, ri: f_ref[s, pos, u1, pl.ds(QRT * ri + 8 * h, 8), :],
                tab_ref, ltab_ref, (2 * u1, 2 * u1 + 1), x, before, after, part, h, store,
            )


def neighbours(sz, slot, first, extent):
    where = first + slot
    before = jnp.where(jnp.logical_or(where == 0, where == extent), sz.zero, slot)
    after = jnp.where(where == extent - 1, sz.middle, slot + 2)
    return before, after, (where >= extent).astype(jnp.int32)


def edge_part(sz, slot, first, extent):
    return (first + slot >= extent).astype(jnp.int32)


def level_one_slots(sz, begin, end, first, extent, *refs):
    def step(slot, carry):
        before, after, part = neighbours(sz, slot, first, extent)
        level_one(sz, *refs, slot + 1, before, after, part)
        return carry

    lax.fori_loop(begin, end, step, 0)


def level_one_middle(sz, low, high, first, extent, *refs):
    before = jnp.clip(extent - first, low + 1, high)
    level_one(sz, *refs, sz.middle, before, sz.zero, 0)


def run_copies(copies, sems):
    handles = [pltpu.make_async_copy(src, dst, sems.at[i]) for i, (src, dst) in enumerate(copies)]
    for handle in handles:
        handle.start()
    for handle in handles:
        handle.wait()


def local_body(sz, extent_ref, kept, mate, par0, par1, own_f, tab2_out, ltab2_out,
               d, f, par1s, par2s, tab, ltab, tab2, ltab2, sems, out_sems):
    core, side, extent, _ = place(extent_ref)
    first = core * sz.slots
    used = sz.used
    run_copies(
        [
            (kept, d.at[core, pl.ds(0, used)]),
            (mate.at[pl.ds(0, used)], d.at[1 - core, pl.ds(0, used)]),
            (par0.at[side], par1s.at[core]),
            (mate.at[used], par1s.at[1 - core]),
            (par1, par2s.at[core]),
            (mate.at[used + 1], par2s.at[1 - core, pl.ds(0, ROW)]),
            (mate.at[used + 2], par2s.at[1 - core, pl.ds(ROW, ROW)]),
        ],
        sems,
    )
    for s in range(2):
        d[s, sz.zero] = jnp.zeros((ROW, BLK), F32)
    build_tables(sz, par1s, tab, ltab, 2, extent, first)
    build_tables(sz, par2s, tab2, ltab2, 4, extent, first)
    refs = (d, f, tab, ltab)
    level_one(sz, *refs, 0, 0, 1, edge_part(sz, 0, first, extent))
    level_one_slots(sz, 0, sz.slots, first, extent, *refs)
    level_one(sz, *refs, sz.right, sz.slots, sz.zero, edge_part(sz, sz.slots - 1, first, extent))
    level_one_middle(sz, 0, sz.slots, first, extent, *refs)
    run_copies([(f, own_f), (tab2, tab2_out), (ltab2, ltab2_out)], out_sems)


def other_tables_body(sz, extent_ref, halo_same, halo_cross, tab_out, ltab_out, pars, tab, ltab, sems):
    core, _, extent, _ = place(extent_ref)
    run_copies([(halo_same.at[3], pars.at[core]), (halo_cross.at[3], pars.at[1 - core])], sems)
    build_tables(sz, pars, tab, ltab, 2, extent, core * sz.slots)
    run_copies([(tab, tab_out), (ltab, ltab_out)], sems)


def main_body(sz, begin, count, passes, extent_ref, *rest):
    head, last = begin == 0, begin + count == sz.slots
    ins = list(rest)
    take = ins.pop
    same, cross, halo_same, halo_cross, own_f, tab1_in, ltab1_in, tab2_in, ltab2_in = ins[:9]
    ins = ins[9:]
    if not head:
        dtail_in, ftail_in, _ = ins[:3]
        ins = ins[3:]
    ins = ins[passes:]
    out = ins[0]
    ins = ins[1:]
    if not last:
        dtail_out, ftail_out = ins[:2]
        ins = ins[2:]
    ins = ins[passes:]
    d, f, tab1, ltab1, tab2, ltab2, o, sems, out_sem = ins
    core, _, extent, _ = place(extent_ref)
    side = place(extent_ref)[1]
    first = core * sz.slots
    end = begin + count
    mine, theirs = core, 1 - core
    low = 0 if head else begin - 2
    copies = [
        (same, d.at[mine, pl.ds(begin + 1, count)]),
        (cross, d.at[theirs, pl.ds(begin + 1, count)]),
        (halo_same.at[pl.ds(1, 2)], d.at[mine, pl.ds(sz.right, 2)]),
        (halo_cross.at[pl.ds(1, 2)], d.at[theirs, pl.ds(sz.right, 2)]),
        (tab1_in, tab1),
        (ltab1_in, ltab1),
        (tab2_in, tab2),
        (ltab2_in, ltab2),
    ]
    fl, fh = max(low - 1, -1) + 1, (end + 1 if last else end)
    copies.append((own_f.at[pl.ds(fl, fh - fl)], f.at[side, pl.ds(fl, fh - fl)]))
    copies.append((own_f.at[sz.middle], f.at[side, sz.middle]))
    if last:
        copies.append((own_f.at[sz.right], f.at[side, sz.right]))
    if head:
        copies.append((halo_same.at[0], d.at[mine, 0]))
        copies.append((halo_cross.at[0], d.at[theirs, 0]))
    else:
        copies.append((dtail_in, d.at[:, pl.ds(begin - 1, 2)]))
        copies.append((ftail_in, f.at[1 - side, pl.ds(begin - 2, 2)]))
    run_copies(copies, sems)
    for s in range(2):
        d[s, sz.zero] = jnp.zeros((ROW, BLK), F32)
        for u in range(2):
            f[s, sz.zero, u] = jnp.zeros((ROW, BLK), F32)
    refs = (d, f.at[1 - side], tab1, ltab1)
    if head:
        level_one(sz, *refs, 0, 0, 1, edge_part(sz, 0, first, extent))
    level_one_slots(sz, 0 if head else begin - 1, end if last else end - 1, first, extent, *refs)
    if last:
        level_one(sz, *refs, sz.right, sz.slots, sz.zero, edge_part(sz, sz.slots - 1, first, extent))
    level_one_middle(sz, low, end, first, extent, *refs)
    top = end if last else end - 2

    def step(slot, carry):
        before, after, part = neighbours(sz, slot, first, extent)
        level_two(sz, f, o, slot - low, tab2, ltab2, slot + 1, before, after, part)
        lanes = pl.ds(pl.multiple_of(slot * BLK, BLK), BLK)
        pltpu.make_async_copy(o.at[slot - low], out.at[:, :, lanes], out_sem).start()
        return carry

    lax.fori_loop(low, top, step, 0)
    if not last:
        run_copies(
            [(d.at[:, pl.ds(end - 1, 2)], dtail_out), (f.at[1 - side, pl.ds(end - 2, 2)], ftail_out)],
            sems,
        )
    pltpu.make_async_copy(o, o, out_sem).wait()


def per_device(images, band_shift, tap_weights, phases, extent_map):
    total_rows = images.shape[2]
    beams = images.shape[1]
    assert beams == 4 * QRT
    slots = total_rows // BLK // 2
    sz = Sizes(slots, total_rows)
    chunks = CHUNKS
    assert sum(chunks) == slots and sz.cols + 6 <= BLK // 2 and sz.zero < BLK
    size = lax.axis_size("sub")
    top = 1 << (size.bit_length() - 2)
    dma = pltpu.SemaphoreType.DMA
    swap = lambda x, by: lax.ppermute(x, "sub", [(i, i ^ by) for i in range(size)])
    block = lambda n: shape(n, 2, QRT, BLK)
    flat = lambda x: x.reshape(x.shape[0], ROW, BLK)

    same0, cross0 = call(
        functools.partial(first_pack, sz), [extent_map, images],
        [block(chunks[0])] * 2, [dma((2,))], 0,
    )
    got = [(flat(swap(same0, top)), flat(swap(cross0, top ^ 1)))]

    par = jnp.concatenate(
        [
            band_shift[0, :, :, :, : sz.cols].astype(F32),
            tap_weights[0],
            phases[0],
            jnp.zeros((2, 2, beams, BLK // 2 - sz.cols - 6), F32),
        ],
        axis=3,
    )
    par = jnp.concatenate([par[:, 0], par[:, 1]], axis=2)
    par0, par1 = (par[i].reshape(2, 2, QRT, BLK) for i in range(2))

    outs = [block(4)] * 2 + [block(sz.used + 3), block(sz.used)]
    for count in chunks[1:]:
        outs += [block(count)] * 2
    packed = call(
        functools.partial(rest_pack, sz, chunks), [extent_map, images, par0, par1],
        outs, [dma((len(outs),))], 0,
    )
    halo = [flat(swap(packed[0], top)), flat(swap(packed[1], top ^ 1))]
    mate = flat(swap(packed[2], 1))
    kept = flat(packed[3])
    got.append((flat(swap(packed[4], top)), flat(swap(packed[5], top ^ 1))))
    waiting = list(packed[6:])

    tabs1, ltabs1 = shape(2, 2, 9, QRT, BLK), shape(2, 2, 2, 2, QRT, BLK)
    tabs2, ltabs2 = shape(2, 4, 9, QRT, BLK), shape(2, 2, 4, 2, QRT, BLK)
    vm = lambda s: pltpu.VMEM(s.shape, F32)
    d_s, f_s = shape(2, sz.zero + 1, ROW, BLK), shape(sz.used, 2, ROW, BLK)
    own_f, tab2, ltab2 = call(
        functools.partial(local_body, sz),
        [extent_map, kept, mate, par0.reshape(2, ROW, BLK), par1.reshape(2 * ROW, BLK)],
        [f_s, tabs2, ltabs2],
        [vm(d_s), vm(f_s), vm(shape(2, ROW, BLK)), vm(shape(2, 2 * ROW, BLK)),
         vm(tabs1), vm(ltabs1), vm(tabs2), vm(ltabs2), dma((7,)), dma((3,))],
        10**8,
    )
    tab1, ltab1 = call(
        functools.partial(other_tables_body, sz), [extent_map] + halo, [tabs1, ltabs1],
        [vm(shape(2, ROW, BLK)), vm(tabs1), vm(ltabs1), dma((2,))], 10**6,
    )

    begin = 0
    out = None
    for k, count in enumerate(chunks):
        head, last = k == 0, k == len(chunks) - 1
        ins = [extent_map, *got[k], *halo, own_f, tab1, ltab1, tab2, ltab2]
        outs = [shape(2, beams, slots * BLK)]
        aliases = {}
        if not head:
            aliases[len(ins) + 2] = 0
            ins += [dtail, ftail, out]
        if not last:
            outs += [shape(2, 2, ROW, BLK), shape(2, 2, ROW, BLK)]
        passes = waiting[:2]
        waiting = waiting[2:]
        for x in passes:
            aliases[len(ins)] = len(outs)
            ins.append(x)
            outs.append(shape(*x.shape))
        low = 0 if head else begin - 2
        done = (begin + count if last else begin + count - 2) - low
        res = call(
            functools.partial(main_body, sz, begin, count, len(passes)), ins, outs,
            [vm(d_s), vm(shape(2, sz.zero + 1, 2, ROW, BLK)), vm(tabs1), vm(ltabs1), vm(tabs2), vm(ltabs2),
             vm(shape(done, 2, beams, BLK)), dma((14,)), dma],
            10**7 * count, aliases,
        )
        out = res[0]
        if not last:
            dtail, ftail = res[1:3]
        if passes:
            same, cross = res[-2:]
            got.append((flat(swap(same, top)), flat(swap(cross, top ^ 1))))
        begin += count
    return out


def solution(mesh):
    placed = (
        P(None, None, ("strip", "sub")),
        P(("strip", "sub"), None, None, None, None),
        P(("strip", "sub"), None, None, None, None),
        P(("strip", "sub"), None, None, None, None),
        P("strip"),
    )
    return jax.shard_map(
        per_device,
        mesh=mesh,
        in_specs=placed,
        out_specs=P(None, None, ("strip", "sub")),
        check_vma=False,
    )
```

```python
import functools

import jax
import jax.numpy as jnp
from jax import lax
from jax.experimental import pallas as pl
from jax.experimental.pallas import tpu as pltpu
from jax.sharding import PartitionSpec as P

BLK = 128
QRT = 16
ROW = 2 * QRT
CHUNKS = (12, 14, 6)

REACH = 10
BASE = (24, 72)


class Sizes:
    def __init__(self, slots, total_rows):
        self.slots = slots
        self.total = total_rows
        self.right = slots + 1
        self.middle = slots + 2
        self.zero = slots + 3
        self.used = slots + 3


F32 = jnp.float32
ANY, HBM, VMEM, SMEM = pl.ANY, pltpu.HBM, pltpu.VMEM, pltpu.SMEM
DMA = pltpu.SemaphoreType.DMA


def shape(*dims):
    return jax.ShapeDtypeStruct(dims, F32)


def call(body, ins, outs, scratch, aliases=None, grant=32):
    return pl.pallas_call(
        body,
        out_shape=tuple(x for x, _ in outs),
        in_specs=[pl.BlockSpec(memory_space=m) for _, m in ins],
        out_specs=tuple(pl.BlockSpec(memory_space=m) for _, m in outs),
        scratch_shapes=scratch,
        input_output_aliases=aliases or {},
        compiler_params=pltpu.CompilerParams(vmem_limit_bytes=grant * 2**20),
        cost_estimate=pl.CostEstimate(flops=1, bytes_accessed=1, transcendentals=0),
    )(*(x for x, _ in ins))


def place(extent_ref):
    pos = lax.axis_index("sub")
    top = lax.axis_size("sub").bit_length() - 2
    core = pos & 1
    side = (pos >> top) & 1
    even = pos - core
    return core, side, extent_ref[even], extent_ref[even ^ (1 << top)]


def copy_block(images_ref, dst, side, part, block, sem):
    rows = pl.ds(pl.multiple_of(part * 2 * QRT + side * QRT, QRT), QRT)
    lanes = pl.ds(pl.multiple_of(block * BLK, BLK), BLK)
    pltpu.make_async_copy(images_ref.at[:, rows, lanes], dst, sem).start()


def copy_slots(images_ref, dst_ref, base, side, extent, first, count, sem):
    def step(i, carry):
        slot = first + i
        part = (slot >= extent).astype(jnp.int32)
        copy_block(images_ref, dst_ref.at[base + i], side, part, slot - part * extent, sem)
        return carry

    lax.fori_loop(0, count, step, 0)


def copy_halo(images_ref, dst_ref, left_at, right_at, middle_at, side, extent, first, slots, sem):
    part = (first >= extent).astype(jnp.int32)
    block = jnp.maximum(first - part * extent - 1, 0)
    copy_block(images_ref, dst_ref.at[left_at], side, part, block, sem)
    last = first + slots - 1
    part = (last >= extent).astype(jnp.int32)
    copy_block(images_ref, dst_ref.at[right_at], side, part, last - part * extent + 1, sem)
    copy_block(images_ref, dst_ref.at[middle_at], side, 0, extent, sem)


def wait_whole(ref, sem):
    pltpu.make_async_copy(ref, ref, sem).wait()


def run_copies(copies, sems):
    handles = [pltpu.make_async_copy(src, dst, sems.at[i]) for i, (src, dst) in enumerate(copies)]
    for handle in handles:
        handle.start()
    for handle in handles:
        handle.wait()


def pack_body(sz, chunks, extent_ref, images_ref, shift_ref, taps_ref, phase_ref, *rest):
    sends = 2 + 2 * len(chunks)
    outs = rest[:sends]
    mate, kept, own_par = outs[-2], outs[-1], rest[sends]
    moved_ref, turned_ref, shifts_ref, edges_ref, made_ref, sems, edge_sem, made_sem = rest[sends + 1 :]
    core, side, own, other = place(extent_ref)
    slots = sz.slots
    windows = (core * slots, (1 - core) * slots)
    for i in range(2):
        copy_halo(images_ref, edges_ref.at[i], 0, 1, 2, 1 - side, other, windows[i], slots, edge_sem)
    begin = 0
    for k, count in enumerate(chunks):
        for i in range(2):
            at = 2 * k + i
            copy_slots(images_ref, outs[at], 0, 1 - side, other, windows[i] + begin, count, sems.at[at])
        begin += count
    for at, ref, window in ((sends - 2, mate, windows[1]), (sends - 1, kept, windows[0])):
        copy_slots(images_ref, ref, 1, side, own, window, slots, sems.at[at])
        copy_halo(images_ref, ref, 0, sz.right, sz.middle, side, own, window, slots, sems.at[at])

    half = BLK // 2
    for l in range(2):
        moved_ref[...] = jnp.zeros((BLK, BLK), F32)
        for s in range(2):
            at = BASE[s] + sz.used
            moved_ref[at : at + 4, 0:half] = taps_ref[l, s]
            moved_ref[at + 4 : at + 6, 0:half] = phase_ref[l, s]
            shifts_ref[l, s] = jnp.zeros((half, BLK), F32)
            shifts_ref[l, s, :, 0:half] = shift_ref[l, s].astype(F32)
        turned_ref[l] = moved_ref[...].T[0:half]
    lane = lax.broadcasted_iota(jnp.int32, (ROW, BLK), 1)

    def parameters(l, row, first, extent):
        rows = pl.ds(pl.multiple_of(row, ROW), ROW)
        result = turned_ref[l, rows, :]
        for s in range(2):
            shifts = shifts_ref[l, s, rows, :]
            at = BASE[s]
            turn = lambda by: pltpu.roll(shifts, jnp.bitwise_and(by, BLK - 1), 1)
            inside = jnp.logical_and(lane >= at, lane < at + sz.middle)
            result = jnp.where(inside, turn(at + 1 - first + core * extent), result)
            result = jnp.where(lane == at + sz.middle, turn(at + sz.middle - extent), result)
        return result

    for i, level, row in ((0, 0, side * ROW), (1, 1, 0), (2, 1, ROW)):
        made_ref[2 + i] = parameters(level, row, windows[1], own).reshape(2, QRT, BLK)
        own_par[i] = parameters(level, row, windows[0], own)
    wait_whole(edges_ref, edge_sem)
    for i in range(2):
        left, right, middle = (edges_ref[i, n].reshape(ROW, BLK) for n in range(3))
        result = parameters(0, (1 - side) * ROW, windows[i], other)
        result = jnp.where(lane < 2 * REACH, pltpu.roll(middle, REACH, 1), result)
        result = jnp.where(lane < REACH, right, result)
        result = jnp.where(lane >= BLK - 2, left, result)
        made_ref[i] = result.reshape(2, QRT, BLK)
        pltpu.make_async_copy(made_ref.at[i], outs[i].at[chunks[0]], made_sem).start()
    pltpu.make_async_copy(made_ref.at[pl.ds(2, 3)], mate.at[pl.ds(sz.used, 3)], made_sem).start()
    wait_whole(made_ref, made_sem)
    for at, ref in enumerate(outs):
        if at < 2:
            ref = ref.at[pl.ds(0, chunks[0])]
        elif at == sends - 2:
            ref = ref.at[pl.ds(0, sz.used)]
        wait_whole(ref, sems.at[at])


def build_tables(sz, par_ref, tab_ref, ltab_ref, groups, extent, first):
    lane = lax.broadcasted_iota(jnp.int32, (QRT, BLK), 1)
    middle = lane == sz.middle
    even = jnp.logical_or(first + lane - 1 < extent, middle)
    block = jnp.where(even, first - 1 + lane, first - 1 + lane - extent)
    block = jnp.where(middle, extent, block).astype(F32)
    for group in range(groups):
        rows = [par_ref[p, pl.ds(group, QRT, stride=groups), :] for p in range(2)]
        for s in range(2):

            def spread(p, n):
                c = BASE[s] + sz.used + n
                return jnp.broadcast_to(rows[p][:, c : c + 1], (QRT, BLK))

            column = lambda n: jnp.where(even, spread(0, n), spread(1, n))
            shift = jnp.where(
                even,
                pltpu.roll(rows[0], BLK - BASE[s], 1),
                pltpu.roll(rows[1], BLK - BASE[s], 1),
            )
            taps = [column(k) for k in range(4)]
            for o in range(-1, 6):
                weight = jnp.zeros((QRT, BLK), F32)
                for k in range(4):
                    if 0 <= o + 1 - k <= 3:
                        weight = weight + jnp.where(shift == float(o + 1 - k), taps[k], 0.0)
                tab_ref[s, group, o + 1] = weight
            angle = column(4) + column(5) * (block * (BLK / sz.total))
            tab_ref[s, group, 7] = jnp.cos(angle)
            tab_ref[s, group, 8] = jnp.sin(angle)
            for p in range(2):
                angle = spread(p, 5) * (lane.astype(F32) / sz.total)
                ltab_ref[p, s, group, 0] = jnp.cos(angle)
                ltab_ref[p, s, group, 1] = jnp.sin(angle)


def gathered(tab_ref, ltab_ref, s, group, x, part, rows):
    pick = jnp.full((8, BLK), x, jnp.int32)
    spread = [jnp.take_along_axis(tab_ref[s, group, k, rows, :], pick, axis=1) for k in range(9)]
    cl = ltab_ref[part, s, group, 0, rows, :]
    sl = ltab_ref[part, s, group, 1, rows, :]
    cosine = spread[7] * cl - spread[8] * sl
    sine = spread[8] * cl + spread[7] * sl
    return spread[:7] + [cosine, sine]


def merge_block(sources, load, coef, sums, x, before, after, store):
    lane = lax.broadcasted_iota(jnp.int32, (8, BLK), 1)
    for s in sources:
        moved = []
        for ri in range(2):
            cur, prv, nxt = load(s, x, ri), load(s, before, ri), load(s, after, ri)
            views = [pltpu.roll(jnp.where(lane == BLK - 1, prv, cur), 1, 1), cur]
            for o in range(1, 6):
                views.append(pltpu.roll(jnp.where(lane < o, nxt, cur), BLK - o, 1))
            moved.append(views)
        for u in range(2):
            *weights, cosine, sine = coef(s, u)
            value = []
            for ri in range(2):
                total = weights[0] * moved[ri][0]
                for k in range(1, 7):
                    total = total + weights[k] * moved[ri][k]
                value.append(total)
            real = cosine * value[0] - sine * value[1]
            imag = sine * value[0] + cosine * value[1]
            sums[u] = [real, imag] if sums[u] is None else [sums[u][0] + real, sums[u][1] + imag]
    for u in range(2):
        for ri in range(2):
            store(u, ri, sums[u][ri])


def level_one(d_ref, f_ref, coef, x, before, after):
    for h in range(2):
        rows = lambda ri: pl.ds(QRT * ri + 8 * h, 8)

        def store(u, ri, value):
            f_ref[x, u, rows(ri), :] = value

        merge_block(
            (0, 1), lambda s, at, ri: d_ref[s, at, rows(ri), :],
            lambda s, u: coef(pl.ds(8 * h, 8), s, u), [None, None], x, before, after, store,
        )


def level_two(f_ref, coef, start, store, x, before, after):
    for u1 in range(2):
        for h in range(2):
            sums = [start(2 * u1 + u, h) for u in range(2)]
            merge_block(
                (0,), lambda s, at, ri: f_ref[at, u1, pl.ds(QRT * ri + 8 * h, 8), :],
                lambda s, u: coef(pl.ds(8 * h, 8), 2 * u1 + u), sums, x, before, after,
                lambda u, ri, value: store(2 * u1 + u, h, ri, value),
            )


def neighbours(sz, slot, first, extent):
    where = first + slot
    before = jnp.where(jnp.logical_or(where == 0, where == extent), sz.zero, slot)
    after = jnp.where(where == extent - 1, sz.middle, slot + 2)
    return before, after, (where >= extent).astype(jnp.int32)


def loop(begin, end, body):
    def step(slot, carry):
        body(slot)
        return carry

    lax.fori_loop(begin, end, step, 0)


def level_one_all(sz, d_ref, f_ref, coef_at, slots, left, right, low, high, first, extent):
    part_of = lambda slot: (first + slot >= extent).astype(jnp.int32)

    def body(slot):
        before, after, part = neighbours(sz, slot, first, extent)
        level_one(d_ref, f_ref, coef_at(slot + 1, part), slot + 1, before, after)

    if left:
        level_one(d_ref, f_ref, coef_at(0, part_of(0)), 0, 0, 1)
    loop(*slots, body)
    if right:
        part = part_of(sz.slots - 1)
        level_one(d_ref, f_ref, coef_at(sz.right, part), sz.right, sz.slots, sz.zero)
    before = jnp.clip(extent - first, low + 1, high)
    level_one(d_ref, f_ref, coef_at(sz.middle, 0), sz.middle, before, sz.zero)


def table_coef(tab, ltab):
    return lambda x, part: (lambda rows, s, u: gathered(tab, ltab, s, u, x, part, rows))


def local_body(sz, extent_ref, kept, mate, par, share_out, tab2_out, ltab2_out,
               d, f, par1s, par2s, tab, ltab, share, tab2, ltab2, sems, out_sems):
    core, side, extent, _ = place(extent_ref)
    first = core * sz.slots
    used = sz.used
    run_copies(
        [
            (kept, d.at[core, pl.ds(0, used)]),
            (mate.at[pl.ds(0, used)], d.at[1 - core, pl.ds(0, used)]),
            (par.at[0], par1s.at[core]),
            (par.at[1], par2s.at[core, pl.ds(0, ROW)]),
            (par.at[2], par2s.at[core, pl.ds(ROW, ROW)]),
            (mate.at[used], par1s.at[1 - core]),
            (mate.at[used + 1], par2s.at[1 - core, pl.ds(0, ROW)]),
            (mate.at[used + 2], par2s.at[1 - core, pl.ds(ROW, ROW)]),
        ],
        sems,
    )
    zeros = jnp.zeros((ROW, BLK), F32)
    for s in range(2):
        d[s, sz.zero] = zeros
        f[sz.zero, s] = zeros
    build_tables(sz, par1s, tab, ltab, 2, extent, first)
    build_tables(sz, par2s, tab2, ltab2, 4, extent, first)
    level_one_all(
        sz, d, f, table_coef(tab, ltab), (0, sz.slots), True, True, 0, sz.slots, first, extent
    )

    def body(slot):
        before, after, part = neighbours(sz, slot, first, extent)

        def store(u, h, ri, value):
            share[slot, ri, u, pl.ds(8 * h, 8), :] = value

        level_two(
            f, lambda rows, u: gathered(tab2, ltab2, side, u, slot + 1, part, rows),
            lambda u, h: None, store, slot + 1, before, after,
        )

    loop(0, sz.slots, body)
    run_copies([(share, share_out), (tab2, tab2_out), (ltab2, ltab2_out)], out_sems)


def other_tables_body(sz, begin, extent_ref, halo_same, halo_cross, tab2, ltab2,
                      tab_out, ltab_out, wide1_out, wide2_out, pars, tab, ltab, wide1, wide2, sems):
    core, side, extent, _ = place(extent_ref)
    first = core * sz.slots
    pars[core] = halo_same[halo_same.shape[0] - 1]
    pars[1 - core] = halo_cross[halo_cross.shape[0] - 1]
    build_tables(sz, pars, tab, ltab, 2, extent, first)
    rows = lambda h: pl.ds(8 * h, 8)

    def spread_one(j, x, part):
        for s in range(2):
            for u in range(2):
                for h in range(2):
                    for k, value in enumerate(gathered(tab, ltab, s, u, x, part, rows(h))):
                        wide1[j, s, u, k, rows(h), :] = value

    def body_one(slot):
        _, _, part = neighbours(sz, slot, first, extent)
        spread_one(slot - begin + 1, slot + 1, part)

    def body_two(slot):
        _, _, part = neighbours(sz, slot, first, extent)
        for u in range(4):
            for h in range(2):
                values = gathered(tab2, ltab2, 1 - side, u, slot + 1, part, rows(h))
                for k, value in enumerate(values):
                    wide2[slot - begin + 2, u, k, rows(h), :] = value

    loop(begin - 1, sz.slots, body_one)
    count = sz.slots - begin
    _, _, part = neighbours(sz, sz.slots - 1, first, extent)
    spread_one(count + 1, sz.right, part)
    spread_one(count + 2, sz.middle, 0)
    loop(begin - 2, sz.slots, body_two)
    run_copies([(tab, tab_out), (ltab, ltab_out), (wide1, wide1_out), (wide2, wide2_out)], sems)


def gate_body(*refs):
    pass


def main_body(sz, begin, count, extent_ref, *rest):
    head, last = begin == 0, begin + count == sz.slots
    ins = list(rest)

    def take(n):
        part = ins[:n]
        del ins[:n]
        return part

    same, cross, halo_same, halo_cross, share = take(5)
    tables = take(2 if last else 4)
    if not head:
        dtail_in, ftail_in, _ = take(3)
    (out,) = take(1)
    if not last:
        dtail_out, ftail_out = take(2)
    d, f, o, out_sem = ins
    core, side, extent, _ = place(extent_ref)
    first = core * sz.slots
    end = begin + count
    low = 0 if head else begin - 2
    zeros = jnp.zeros((ROW, BLK), F32)
    for mine, chunk, halo in ((core, same, halo_same), (1 - core, cross, halo_cross)):
        for i in range(count):
            d[mine, begin + 1 + i] = chunk[i]
        edge = halo[halo.shape[0] - 1]
        if head:
            d[mine, 0] = edge
        if last:
            d[mine, sz.right] = edge
        d[mine, sz.middle] = pltpu.roll(edge, BLK - REACH, 1)
    for s in range(2):
        d[s, sz.zero] = zeros
        f[sz.zero, s] = zeros
        if not head:
            for i in range(2):
                d[s, begin - 1 + i] = dtail_in[s, i]
                f[begin - 2 + i, s] = ftail_in[i, s]

    if last:
        wide1, wide2 = tables

        def coef_at(x, part):
            if isinstance(x, int):
                j = count + 1 if x == sz.right else count + 2
            else:
                j = x - begin
            return lambda rows, s, u: [wide1[j, s, u, k, rows, :] for k in range(9)]
    else:
        tab1, ltab1, tab2, ltab2 = tables
        coef_at = table_coef(tab1, ltab1)
    slots = (0 if head else begin - 1, end if last else end - 1)
    level_one_all(sz, d, f, coef_at, slots, head, last, low, end, first, extent)

    def body(slot):
        before, after, part = neighbours(sz, slot, first, extent)
        at = slot - low

        def store(u, h, ri, value):
            o[at, ri, pl.ds(32 * h + u, 8, stride=4), :] = value

        if last:
            coef = lambda rows, u: [wide2[at, u, k, rows, :] for k in range(9)]
        else:
            coef = lambda rows, u: gathered(tab2, ltab2, 1 - side, u, slot + 1, part, rows)
        level_two(
            f, coef, lambda u, h: [share[slot, ri, u, pl.ds(8 * h, 8), :] for ri in range(2)],
            store, slot + 1, before, after,
        )
        lanes = pl.ds(pl.multiple_of(slot * BLK, BLK), BLK)
        pltpu.make_async_copy(o.at[at], out.at[:, :, lanes], out_sem).start()

    loop(low, end if last else end - 2, body)
    if not last:
        for s in range(2):
            for i in range(2):
                dtail_out[s, i] = d[s, end - 1 + i]
                ftail_out[i, s] = f[end - 2 + i, s]
    wait_whole(o, out_sem)


def per_device(images, band_shift, tap_weights, phases, extent_map):
    total_rows = images.shape[2]
    beams = images.shape[1]
    slots = total_rows // BLK // 2
    sz = Sizes(slots, total_rows)
    chunks = CHUNKS
    assert beams == 4 * QRT and sum(chunks) == slots and len(chunks) == 3
    assert sz.used + 6 <= BASE[1] - BASE[0] and BASE[1] + sz.used + 6 <= BLK - 2
    size = lax.axis_size("sub")
    top = 1 << (size.bit_length() - 2)
    swap = lambda x, by: lax.ppermute(x, "sub", [(i, i ^ by) for i in range(size)])
    block = lambda n: (shape(n, 2, QRT, BLK), VMEM)
    flat = lambda x: x.reshape(x.shape[0], ROW, BLK)
    extents = (extent_map, SMEM)
    vm = lambda *dims: VMEM(dims, F32)

    outs = [block(chunks[0] + 1)] * 2
    for count in chunks[1:]:
        outs += [block(count)] * 2
    outs += [block(sz.used + 3), block(sz.used), (shape(3, ROW, BLK), VMEM)]
    half = BLK // 2
    packed = call(
        functools.partial(pack_body, sz, chunks),
        [
            extents,
            (images, HBM),
            (band_shift[0], VMEM),
            (tap_weights[0].transpose(0, 1, 3, 2), VMEM),
            (phases[0].transpose(0, 1, 3, 2), VMEM),
        ],
        outs,
        [vm(BLK, BLK), vm(2, half, BLK), vm(2, 2, half, BLK), vm(2, 3, 2, QRT, BLK),
         vm(5, 2, QRT, BLK), DMA((len(outs),)), DMA, DMA],
        grant=56,
    )
    send = lambda a, b: (flat(swap(a, top)), flat(swap(b, top ^ 1)))
    got = [send(*packed[0:2]), send(*packed[2:4])]
    mate, kept, own_par = flat(swap(packed[6], 1)), flat(packed[7]), packed[8]
    halo = [(x, VMEM) for x in got[0]]

    tabs1, ltabs1 = (2, 2, 9, QRT, BLK), (2, 2, 2, 2, QRT, BLK)
    tabs2, ltabs2 = (2, 4, 9, QRT, BLK), (2, 2, 4, 2, QRT, BLK)
    shares = (slots, 2, 4, QRT, BLK)
    d_s, f_s = (2, sz.zero + 1, ROW, BLK), (sz.zero + 1, 2, ROW, BLK)
    share, tab2, ltab2 = call(
        functools.partial(local_body, sz),
        [extents, (kept, ANY), (mate, ANY), (own_par, ANY)],
        [(shape(*shares), ANY), (shape(*tabs2), ANY), (shape(*ltabs2), ANY)],
        [vm(*d_s), vm(*f_s), vm(2, ROW, BLK), vm(2, 2 * ROW, BLK), vm(*tabs1), vm(*ltabs1),
         vm(*shares), vm(*tabs2), vm(*ltabs2), DMA((8,)), DMA((3,))],
    )
    count = chunks[-1]
    wides1, wides2 = (count + 3, 2, 2, 9, QRT, BLK), (count + 2, 4, 9, QRT, BLK)
    tab1, ltab1, wide1, wide2 = call(
        functools.partial(other_tables_body, sz, slots - count),
        [extents, *halo, (tab2, VMEM), (ltab2, VMEM)],
        [(shape(*s), ANY) for s in (tabs1, ltabs1, wides1, wides2)],
        [vm(2, ROW, BLK), vm(*tabs1), vm(*ltabs1), vm(*wides1), vm(*wides2), DMA((4,))],
    )

    waiting = [(x, ANY) for x in packed[4:6]]
    opened = call(
        gate_body, waiting + [(x, ANY) for x in got[0]] + [(share, ANY)],
        waiting, [], {0: 0, 1: 1},
    )
    got.append(send(*opened))

    begin = 0
    tail = [(shape(2, 2, ROW, BLK), VMEM)] * 2
    for k, count in enumerate(chunks):
        head, last = k == 0, k == len(chunks) - 1
        ins = [extents, *((x, VMEM) for x in got[k]), *halo, (share, VMEM)]
        if last:
            ins += [(wide1, VMEM), (wide2, VMEM)]
        else:
            ins += [(x, VMEM) for x in (tab1, ltab1, tab2, ltab2)]
        outs = [(shape(2, beams, slots * BLK), HBM)]
        aliases = {}
        if not head:
            aliases[len(ins) + 2] = 0
            ins += [(dtail, VMEM), (ftail, VMEM), (out, HBM)]
        if not last:
            outs += tail
        low = 0 if head else begin - 2
        done = (begin + count if last else begin + count - 2) - low
        res = call(
            functools.partial(main_body, sz, begin, count), ins, outs,
            [vm(*d_s), vm(*f_s), vm(done, 2, beams, BLK), DMA], aliases,
        )
        out = res[0]
        if not last:
            dtail, ftail = res[1:]
        begin += count
    return out


def solution(mesh):
    placed = (
        P(None, None, ("strip", "sub")),
        P(("strip", "sub"), None, None, None, None),
        P(("strip", "sub"), None, None, None, None),
        P(("strip", "sub"), None, None, None, None),
        P("strip"),
    )
    return jax.shard_map(
        per_device,
        mesh=mesh,
        in_specs=placed,
        out_specs=P(None, None, ("strip", "sub")),
        check_vma=False,
    )
```

```python
import functools

import jax
import jax.numpy as jnp
from jax import lax
from jax.experimental import pallas as pl
from jax.experimental.pallas import tpu as pltpu
from jax.sharding import PartitionSpec as P

BLK = 128
QRT = 16
ROW = 2 * QRT
CHUNKS = (8, 10, 8, 6)
HINT = 0.5
WIDE = 3

REACH = 10
BASE = (24, 72)


class Sizes:
    def __init__(self, slots, total_rows):
        self.slots = slots
        self.total = total_rows
        self.right = slots + 1
        self.middle = slots + 2
        self.zero = slots + 3
        self.used = slots + 3


F32 = jnp.float32
ANY, HBM, VMEM, SMEM = pl.ANY, pltpu.HBM, pltpu.VMEM, pltpu.SMEM
DMA = pltpu.SemaphoreType.DMA


def shape(*dims):
    return jax.ShapeDtypeStruct(dims, F32)


def call(body, ins, outs, scratch, aliases=None, grant=32, us=0):
    return pl.pallas_call(
        body,
        out_shape=tuple(x for x, _ in outs),
        in_specs=[pl.BlockSpec(memory_space=m) for _, m in ins],
        out_specs=tuple(pl.BlockSpec(memory_space=m) for _, m in outs),
        scratch_shapes=scratch,
        input_output_aliases=aliases or {},
        compiler_params=pltpu.CompilerParams(vmem_limit_bytes=grant * 2**20),
        cost_estimate=pl.CostEstimate(flops=int(us * 10**9) + 1, bytes_accessed=int(us * 3 * 10**6) + 1, transcendentals=0),
    )(*(x for x, _ in ins))


def place(extent_ref):
    pos = lax.axis_index("sub")
    top = lax.axis_size("sub").bit_length() - 2
    core = pos & 1
    side = (pos >> top) & 1
    even = pos - core
    return core, side, extent_ref[even], extent_ref[even ^ (1 << top)]


def wait_whole(ref, sem):
    pltpu.make_async_copy(ref, ref, sem).wait()


def run_copies(copies, sems):
    handles = [pltpu.make_async_copy(src, dst, sems.at[i]) for i, (src, dst) in enumerate(copies)]
    for handle in handles:
        handle.start()
    for handle in handles:
        handle.wait()


def pack_body(sz, chunks, extent_ref, images_ref, shift_ref, taps_ref, phase_ref, *rest):
    sends = 2 + 2 * len(chunks)
    homes, own_par = rest[:sends], rest[sends]
    outs = rest[sends + 1 : 2 * sends + 1]
    mate, kept = outs[-2:]
    field_ref, moved_ref, turned_ref, shifts_ref, raw_ref, pieces_ref, angles_ref, sems, out_sems = rest[2 * sends + 1 :]
    core, side, own, other = place(extent_ref)
    slots = sz.slots
    windows = (core * slots, (1 - core) * slots)
    lanes = field_ref.shape[-1]
    small = [(shift_ref, raw_ref), (taps_ref, pieces_ref), (phase_ref, angles_ref)]
    loads = [pltpu.make_async_copy(*pair, sems.at[4 + i]) for i, pair in enumerate(small)]
    for t, which in enumerate((1 - side, side)):
        for part in range(2):
            rows = pl.ds(pl.multiple_of(part * ROW + which * QRT, QRT), QRT)
            source = images_ref.at[:, rows, pl.ds(0, lanes)]
            loads.append(pltpu.make_async_copy(source, field_ref.at[t, part], sems.at[2 * t + part]))
    for load in loads:
        load.start()
    for load in loads[:3]:
        load.wait()
    stores = [pltpu.make_async_copy(outs[i], homes[i], out_sems.at[i]) for i in range(sends)]

    half = BLK // 2
    for l in range(2):
        moved_ref[...] = jnp.zeros((BLK, BLK), F32)
        for s in range(2):
            at = BASE[s] + sz.used
            moved_ref[at : at + 4, 0:half] = pieces_ref[l, s]
            moved_ref[at + 4 : at + 6, 0:half] = angles_ref[l, s]
            shifts_ref[l, s] = jnp.zeros((half, BLK), F32)
            shifts_ref[l, s, :, 0:half] = raw_ref[l, s].astype(F32)
        turned_ref[l] = moved_ref[...].T[0:half]
    lane = lax.broadcasted_iota(jnp.int32, (ROW, BLK), 1)

    def parameters(l, row, first, extent):
        rows = pl.ds(pl.multiple_of(row, ROW), ROW)
        result = turned_ref[l, rows, :]
        for s in range(2):
            shifts = shifts_ref[l, s, rows, :]
            at = BASE[s]
            turn = lambda by: pltpu.roll(shifts, jnp.bitwise_and(by, BLK - 1), 1)
            inside = jnp.logical_and(lane >= at, lane < at + sz.middle)
            result = jnp.where(inside, turn(at + 1 - first + core * extent), result)
            result = jnp.where(lane == at + sz.middle, turn(at + sz.middle - extent), result)
        return result

    def read(t, part, block):
        return field_ref[t, part, :, :, pl.ds(pl.multiple_of(block * BLK, BLK), BLK)]

    def packed(t, extent, slot):
        part = (slot >= extent).astype(jnp.int32)
        return read(t, part, slot - part * extent)

    def halo(t, extent, first):
        part = (first >= extent).astype(jnp.int32)
        left = read(t, part, jnp.maximum(first - part * extent - 1, 0))
        last = first + slots - 1
        part = (last >= extent).astype(jnp.int32)
        return left, read(t, part, last - part * extent + 1), read(t, 0, extent)

    for i, level, row in ((0, 0, side * ROW), (1, 1, 0), (2, 1, ROW)):
        mate[sz.used + i] = parameters(level, row, windows[1], own).reshape(2, QRT, BLK)
        own_par[i] = parameters(level, row, windows[0], own)
    for load in loads[3:5]:
        load.wait()
    for i in range(2):
        left, right, middle = (x.reshape(ROW, BLK) for x in halo(0, other, windows[i]))
        result = parameters(0, (1 - side) * ROW, windows[i], other)
        result = jnp.where(lane < 2 * REACH, pltpu.roll(middle, REACH, 1), result)
        result = jnp.where(lane < REACH, right, result)
        result = jnp.where(lane >= BLK - 2, left, result)
        outs[i][chunks[0]] = result.reshape(2, QRT, BLK)
        slot = windows[i]
        for k, count in enumerate(chunks):
            for j in range(count):
                outs[2 * k + i][j] = packed(0, other, slot)
                slot = slot + 1
            stores[2 * k + i].start()
    for load in loads[5:]:
        load.wait()
    for n, first in ((sends - 2, windows[1]), (sends - 1, windows[0])):
        ref = outs[n]
        ref[0], ref[sz.right], ref[sz.middle] = halo(1, own, first)
        for j in range(slots):
            ref[1 + j] = packed(1, own, first + j)
        stores[n].start()
    for store in stores:
        store.wait()


def build_tables(sz, par_ref, tab_ref, ltab_ref, groups, extent, first):
    lane = lax.broadcasted_iota(jnp.int32, (QRT, BLK), 1)
    middle = lane == sz.middle
    even = jnp.logical_or(first + lane - 1 < extent, middle)
    block = jnp.where(even, first - 1 + lane, first - 1 + lane - extent)
    block = jnp.where(middle, extent, block).astype(F32)
    for group in range(groups):
        rows = [par_ref[p, pl.ds(group, QRT, stride=groups), :] for p in range(2)]
        for s in range(2):

            def spread(p, n):
                c = BASE[s] + sz.used + n
                return jnp.broadcast_to(rows[p][:, c : c + 1], (QRT, BLK))

            column = lambda n: jnp.where(even, spread(0, n), spread(1, n))
            tab_ref[s, group, 0] = jnp.where(
                even,
                pltpu.roll(rows[0], BLK - BASE[s], 1),
                pltpu.roll(rows[1], BLK - BASE[s], 1),
            )
            angle = column(4) + column(5) * (block * (BLK / sz.total))
            tab_ref[s, group, 1] = jnp.cos(angle)
            tab_ref[s, group, 2] = jnp.sin(angle)
            for p in range(2):
                angle = spread(p, 5) * (lane.astype(F32) / sz.total)
                ltab_ref[p, s, group, 0] = jnp.cos(angle)
                ltab_ref[p, s, group, 1] = jnp.sin(angle)
                for k in range(4):
                    ltab_ref[p, s, group, 2 + k] = spread(p, k)


def gathered(tab_ref, ltab_ref, s, group, x, part, rows):
    pick = jnp.full((8, BLK), x, jnp.int32)
    shift, cb, sb = (
        jnp.take_along_axis(tab_ref[s, group, k, rows, :], pick, axis=1) for k in range(3)
    )
    cl, sl, *taps = (ltab_ref[part, s, group, k, rows, :] for k in range(6))
    two = shift > 1.5
    one = jnp.where(two, shift - 2.0, shift) > 0.5
    zero = jnp.zeros((8, BLK), F32)
    taps = [zero] + taps + [zero]
    taps = [zero] * 2 + [jnp.where(one, taps[k], taps[k + 1]) for k in range(5)] + [zero] * 2
    weights = [jnp.where(two, taps[k], taps[k + 2]) for k in range(7)]
    return weights + [cb * cl - sb * sl, sb * cl + cb * sl]


def merge_block(sources, load, coef, sums, x, before, after, store):
    lane = lax.broadcasted_iota(jnp.int32, (8, BLK), 1)
    for s in sources:
        moved = []
        for ri in range(2):
            cur, prv, nxt = load(s, x, ri), load(s, before, ri), load(s, after, ri)
            views = [pltpu.roll(jnp.where(lane == BLK - 1, prv, cur), 1, 1), cur]
            for o in range(1, 6):
                views.append(pltpu.roll(jnp.where(lane < o, nxt, cur), BLK - o, 1))
            moved.append(views)
        for u in range(2):
            *weights, cosine, sine = coef(s, u)
            value = []
            for ri in range(2):
                total = weights[0] * moved[ri][0]
                for k in range(1, 7):
                    total = total + weights[k] * moved[ri][k]
                value.append(total)
            real = cosine * value[0] - sine * value[1]
            imag = sine * value[0] + cosine * value[1]
            sums[u] = [real, imag] if sums[u] is None else [sums[u][0] + real, sums[u][1] + imag]
    for u in range(2):
        for ri in range(2):
            store(u, ri, sums[u][ri])


def level_one(d_ref, f_ref, coef, x, before, after):
    for h in range(2):
        rows = lambda ri: pl.ds(QRT * ri + 8 * h, 8)

        def store(u, ri, value):
            f_ref[x, u, rows(ri), :] = value

        merge_block(
            (0, 1), lambda s, at, ri: d_ref[s, at, rows(ri), :],
            lambda s, u: coef(pl.ds(8 * h, 8), s, u), [None, None], x, before, after, store,
        )


def level_two(f_ref, coef, start, store, x, before, after):
    for u1 in range(2):
        for h in range(2):
            sums = [start(2 * u1 + u, h) for u in range(2)]
            merge_block(
                (0,), lambda s, at, ri: f_ref[at, u1, pl.ds(QRT * ri + 8 * h, 8), :],
                lambda s, u: coef(pl.ds(8 * h, 8), 2 * u1 + u), sums, x, before, after,
                lambda u, ri, value: store(2 * u1 + u, h, ri, value),
            )


def neighbours(sz, slot, first, extent):
    where = first + slot
    before = jnp.where(jnp.logical_or(where == 0, where == extent), sz.zero, slot)
    after = jnp.where(where == extent - 1, sz.middle, slot + 2)
    return before, after, (where >= extent).astype(jnp.int32)


def loop(begin, end, body):
    def step(slot, carry):
        body(slot)
        return carry

    lax.fori_loop(begin, end, step, 0)


def level_one_all(sz, d_ref, f_ref, coef_at, slots, left, right, low, high, first, extent):
    part_of = lambda slot: (first + slot >= extent).astype(jnp.int32)

    def body(slot):
        before, after, part = neighbours(sz, slot, first, extent)
        level_one(d_ref, f_ref, coef_at(slot + 1, part), slot + 1, before, after)

    if left:
        level_one(d_ref, f_ref, coef_at(0, part_of(0)), 0, 0, 1)
    loop(*slots, body)
    if right:
        part = part_of(sz.slots - 1)
        level_one(d_ref, f_ref, coef_at(sz.right, part), sz.right, sz.slots, sz.zero)
    before = jnp.clip(extent - first, low + 1, high)
    level_one(d_ref, f_ref, coef_at(sz.middle, 0), sz.middle, before, sz.zero)


def table_coef(tab, ltab):
    return lambda x, part: (lambda rows, s, u: gathered(tab, ltab, s, u, x, part, rows))


def local_body(sz, extent_ref, kept, mate, par, f_out, tab2_out, ltab2_out,
               d, f, par1s, par2s, tab, ltab, tab2, ltab2, sems, out_sems):
    core, side, extent, _ = place(extent_ref)
    first = core * sz.slots
    used = sz.used
    run_copies(
        [
            (kept, d.at[core, pl.ds(0, used)]),
            (mate.at[pl.ds(0, used)], d.at[1 - core, pl.ds(0, used)]),
            (par.at[0], par1s.at[core]),
            (par.at[1], par2s.at[core, pl.ds(0, ROW)]),
            (par.at[2], par2s.at[core, pl.ds(ROW, ROW)]),
            (mate.at[used], par1s.at[1 - core]),
            (mate.at[used + 1], par2s.at[1 - core, pl.ds(0, ROW)]),
            (mate.at[used + 2], par2s.at[1 - core, pl.ds(ROW, ROW)]),
        ],
        sems,
    )
    zeros = jnp.zeros((ROW, BLK), F32)
    for s in range(2):
        d[s, sz.zero] = zeros
        f[sz.zero, s] = zeros
    build_tables(sz, par1s, tab, ltab, 2, extent, first)
    build_tables(sz, par2s, tab2, ltab2, 4, extent, first)
    level_one_all(
        sz, d, f, table_coef(tab, ltab), (0, sz.slots), True, True, 0, sz.slots, first, extent
    )
    run_copies([(f, f_out), (tab2, tab2_out), (ltab2, ltab2_out)], out_sems)


def share_body(sz, extent_ref, f, tab2, ltab2, _, share_out, share, sem):
    core, side, extent, _ = place(extent_ref)
    first = core * sz.slots

    def body(slot):
        before, after, part = neighbours(sz, slot, first, extent)

        def store(u, h, ri, value):
            share[slot, ri, u, pl.ds(8 * h, 8), :] = value

        level_two(
            f, lambda rows, u: gathered(tab2, ltab2, side, u, slot + 1, part, rows),
            lambda u, h: None, store, slot + 1, before, after,
        )

    loop(0, sz.slots, body)
    run_copies([(share, share_out)], sem)


def one_range(sz, begin, count):
    end = begin + count
    return (0 if begin == 0 else begin - 1), (end if end == sz.slots else end - 1)


def two_range(sz, begin, count):
    end = begin + count
    return (0 if begin == 0 else begin - 2), (end if end == sz.slots else end - 2)


def other_tables_body(sz, spans, extent_ref, halo_same, halo_cross, tab2, ltab2, tab, ltab, *rest):
    wides, pars = rest[:-1], rest[-1]
    core, side, extent, _ = place(extent_ref)
    first = core * sz.slots
    pars[core] = halo_same[halo_same.shape[0] - 1]
    pars[1 - core] = halo_cross[halo_cross.shape[0] - 1]
    build_tables(sz, pars, tab, ltab, 2, extent, first)
    rows = lambda h: pl.ds(8 * h, 8)
    for n, span in enumerate(spans):
        wide1, wide2 = wides[2 * n : 2 * n + 2]
        one, two = one_range(sz, *span), two_range(sz, *span)

        def spread_one(j, x, part):
            for s in range(2):
                for u in range(2):
                    for h in range(2):
                        values = gathered(tab, ltab, s, u, x, part, rows(h))
                        for k, value in enumerate(values):
                            wide1[j, s, u, k, rows(h), :] = value

        def body_one(slot):
            _, _, part = neighbours(sz, slot, first, extent)
            spread_one(slot - one[0], slot + 1, part)

        def body_two(slot):
            _, _, part = neighbours(sz, slot, first, extent)
            for u in range(4):
                for h in range(2):
                    values = gathered(tab2, ltab2, 1 - side, u, slot + 1, part, rows(h))
                    for k, value in enumerate(values):
                        wide2[slot - two[0], u, k, rows(h), :] = value

        loop(*one, body_one)
        _, _, part = neighbours(sz, sz.slots - 1, first, extent)
        count = one[1] - one[0]
        spread_one(count, sz.middle, 0)
        if one[1] == sz.slots:
            spread_one(count + 1, sz.right, part)
        loop(*two, body_two)


def gate_body(*refs):
    pass


def main_body(sz, begin, count, wide, extent_ref, *rest):
    head, last = begin == 0, begin + count == sz.slots
    ins = list(rest)

    def take(n):
        part = ins[:n]
        del ins[:n]
        return part

    same, cross, halo_same, halo_cross, share = take(5)
    tables = take(2 if wide else 4)
    if not head:
        dtail_in, ftail_in, _ = take(3)
    (out,) = take(1)
    if not last:
        dtail_out, ftail_out = take(2)
    d, f, o, out_sem = ins
    core, side, extent, _ = place(extent_ref)
    first = core * sz.slots
    end = begin + count
    low = 0 if head else begin - 2
    zeros = jnp.zeros((ROW, BLK), F32)
    for mine, chunk, halo in ((core, same, halo_same), (1 - core, cross, halo_cross)):
        for i in range(count):
            d[mine, begin + 1 + i] = chunk[i]
        edge = halo[halo.shape[0] - 1]
        if head:
            d[mine, 0] = edge
        if last:
            d[mine, sz.right] = edge
        d[mine, sz.middle] = pltpu.roll(edge, BLK - REACH, 1)
    for s in range(2):
        d[s, sz.zero] = zeros
        f[sz.zero, s] = zeros
        if not head:
            for i in range(2):
                d[s, begin - 1 + i] = dtail_in[s, i]
                f[begin - 2 + i, s] = ftail_in[i, s]

    slots = one_range(sz, begin, count)
    if wide:
        wide1, wide2 = tables

        def coef_at(x, part):
            if isinstance(x, int):
                j = slots[1] - slots[0] + (1 if x == sz.right else 0)
            else:
                j = x - 1 - slots[0]
            return lambda rows, s, u: [wide1[j, s, u, k, rows, :] for k in range(9)]
    else:
        tab1, ltab1, tab2, ltab2 = tables
        coef_at = table_coef(tab1, ltab1)
    level_one_all(sz, d, f, coef_at, slots, head, last, low, end, first, extent)

    def body(slot):
        before, after, part = neighbours(sz, slot, first, extent)
        at = slot - low

        def store(u, h, ri, value):
            o[at, ri, pl.ds(32 * h + u, 8, stride=4), :] = value

        if wide:
            coef = lambda rows, u: [wide2[at, u, k, rows, :] for k in range(9)]
        else:
            coef = lambda rows, u: gathered(tab2, ltab2, 1 - side, u, slot + 1, part, rows)
        level_two(
            f, coef, lambda u, h: [share[slot, ri, u, pl.ds(8 * h, 8), :] for ri in range(2)],
            store, slot + 1, before, after,
        )
        lanes = pl.ds(pl.multiple_of(slot * BLK, BLK), BLK)
        pltpu.make_async_copy(o.at[at], out.at[:, :, lanes], out_sem).start()

    loop(*two_range(sz, begin, count), body)
    if not last:
        for s in range(2):
            for i in range(2):
                dtail_out[s, i] = d[s, end - 1 + i]
                ftail_out[i, s] = f[end - 2 + i, s]
    wait_whole(o, out_sem)


def per_device(images, band_shift, tap_weights, phases, extent_map):
    total_rows = images.shape[2]
    beams = images.shape[1]
    slots = total_rows // BLK // 2
    sz = Sizes(slots, total_rows)
    chunks = CHUNKS
    assert beams == 4 * QRT and sum(chunks) == slots and len(chunks) > 2
    assert sz.used + 6 <= BASE[1] - BASE[0] and BASE[1] + sz.used + 6 <= BLK - 2
    size = lax.axis_size("sub")
    top = 1 << (size.bit_length() - 2)
    swap = lambda x, by: lax.ppermute(x, "sub", [(i, i ^ by) for i in range(size)])
    flat = lambda x: x.reshape(x.shape[0], ROW, BLK)
    extents = (extent_map, SMEM)
    vm = lambda *dims: VMEM(dims, F32)

    counts = [chunks[0] + 1] * 2
    for count in chunks[1:]:
        counts += [count] * 2
    counts += [sz.used + 3, sz.used]
    half = BLK // 2
    packed = call(
        functools.partial(pack_body, sz, chunks),
        [
            extents,
            (images, HBM),
            (band_shift[0], HBM),
            (tap_weights[0].transpose(0, 1, 3, 2), HBM),
            (phases[0].transpose(0, 1, 3, 2), HBM),
        ],
        [(shape(n, 2, QRT, BLK), ANY) for n in counts] + [(shape(3, ROW, BLK), VMEM)],
        [vm(n, 2, QRT, BLK) for n in counts]
        + [vm(2, 2, 2, QRT, (3 * slots // 2 + 1) * BLK), vm(BLK, BLK), vm(2, half, BLK),
           vm(2, 2, half, BLK), VMEM((2, 2, half, half), jnp.int32), vm(2, 2, 4, half),
           vm(2, 2, 2, half), DMA((7,)), DMA((len(counts),))],
        grant=56,
    )
    send = lambda a, b: (flat(swap(a, top)), flat(swap(b, top ^ 1)))
    def gate(waiting, needed):
        passed = [(x, ANY) for x in waiting]
        out = call(gate_body, passed + [(x, ANY) for x in needed], passed, [], {0: 0, 1: 1})
        return send(*out)

    got = [send(*packed[0:2])]
    last = len(chunks)
    mate, kept, own_par = flat(swap(packed[2 * last], 1)), flat(packed[2 * last + 1]), packed[-1]
    got.append(gate(packed[2:4], [mate]))
    halo = [(x, VMEM) for x in got[0]]

    tabs1, ltabs1 = (2, 2, 3, QRT, BLK), (2, 2, 2, 6, QRT, BLK)
    tabs2, ltabs2 = (2, 4, 3, QRT, BLK), (2, 2, 4, 6, QRT, BLK)
    shares = (slots, 2, 4, QRT, BLK)
    d_s, f_s = (2, sz.zero + 1, ROW, BLK), (sz.zero + 1, 2, ROW, BLK)
    own_f, tab2, ltab2 = call(
        functools.partial(local_body, sz),
        [extents, (kept, HBM), (mate, HBM), (own_par, HBM)],
        [(shape(*f_s), ANY), (shape(*tabs2), ANY), (shape(*ltabs2), ANY)],
        [vm(*d_s), vm(*f_s), vm(2, ROW, BLK), vm(2, 2 * ROW, BLK), vm(*tabs1), vm(*ltabs1),
         vm(*tabs2), vm(*ltabs2), DMA((8,)), DMA((3,))],
        us=10,
    )

    begins = [sum(chunks[:k]) for k in range(len(chunks))]
    spans = [(begins[k], chunks[k]) for k in range(WIDE, len(chunks))]
    outs = [tabs1, ltabs1]
    for span in spans:
        one, two = one_range(sz, *span), two_range(sz, *span)
        extra = 2 if one[1] == slots else 1
        outs += [(one[1] - one[0] + extra, 2, 2, 9, QRT, BLK), (two[1] - two[0], 4, 9, QRT, BLK)]
    got.append(gate(packed[4:6], [*got[0], own_f]))
    tab1, ltab1, *wides = call(
        functools.partial(other_tables_body, sz, spans),
        [extents, *halo, (tab2, VMEM), (ltab2, VMEM)],
        [(shape(*s), VMEM) for s in outs], [vm(2, ROW, BLK)], us=HINT,
    )
    (share,) = call(
        functools.partial(share_body, sz),
        [extents, (own_f, VMEM), (tab2, VMEM), (ltab2, VMEM), (tab1, ANY)],
        [(shape(*shares), ANY)], [vm(*shares), DMA((1,))], us=HINT,
    )

    tail = [(shape(2, 2, ROW, BLK), VMEM)] * 2
    out = None
    for k, count in enumerate(chunks):
        begin = begins[k]
        head, last = k == 0, k == len(chunks) - 1
        if k >= 1 and k + 2 < len(chunks):
            got.append(gate(packed[2 * k + 4 : 2 * k + 6], [*got[k], dtail]))
        ins = [extents, *((x, VMEM) for x in got[k]), *halo, (share, VMEM)]
        if k >= WIDE:
            ins += [(x, VMEM) for x in wides[2 * (k - WIDE) : 2 * (k - WIDE) + 2]]
        else:
            ins += [(x, VMEM) for x in (tab1, ltab1, tab2, ltab2)]
        outs = [(shape(2, beams, slots * BLK), HBM)]
        aliases = {}
        if not head:
            aliases[len(ins) + 2] = 0
            ins += [(dtail, VMEM), (ftail, VMEM), (out, HBM)]
        if not last:
            outs += tail
        low, top_slot = two_range(sz, begin, count)
        res = call(
            functools.partial(main_body, sz, begin, count, k >= WIDE), ins, outs,
            [vm(*d_s), vm(*f_s), vm(top_slot - low, 2, beams, BLK), DMA], aliases, us=HINT if head else 0.1,
        )
        out = res[0]
        if not last:
            dtail, ftail = res[1:]
    return out


def solution(mesh):
    placed = (
        P(None, None, ("strip", "sub")),
        P(("strip", "sub"), None, None, None, None),
        P(("strip", "sub"), None, None, None, None),
        P(("strip", "sub"), None, None, None, None),
        P("strip"),
    )
    return jax.shard_map(
        per_device,
        mesh=mesh,
        in_specs=placed,
        out_specs=P(None, None, ("strip", "sub")),
        check_vma=False,
    )
```

```python
import functools

import jax
import jax.numpy as jnp
from jax import lax
from jax.experimental import pallas as pl
from jax.experimental.pallas import tpu as pltpu
from jax.sharding import PartitionSpec as P

BLK = 128
QRT = 16
ROW = 2 * QRT
CHUNKS = (19, 8, 5)
HINT = 0
LOCAL = 0
MATES = 3
GATED = True
WIDE = 2

REACH = 10
BASE = (24, 72)


class Sizes:
    def __init__(self, slots, total_rows):
        self.slots = slots
        self.total = total_rows
        self.right = slots + 1
        self.middle = slots + 2
        self.zero = slots + 3
        self.used = slots + 3


F32 = jnp.float32
ANY, HBM, VMEM, SMEM = pl.ANY, pltpu.HBM, pltpu.VMEM, pltpu.SMEM
DMA = pltpu.SemaphoreType.DMA


def shape(*dims):
    return jax.ShapeDtypeStruct(dims, F32)


def call(body, ins, outs, scratch, aliases=None, grant=32, us=0):
    return pl.pallas_call(
        body,
        out_shape=tuple(x for x, _ in outs),
        in_specs=[pl.BlockSpec(memory_space=m) for _, m in ins],
        out_specs=tuple(pl.BlockSpec(memory_space=m) for _, m in outs),
        scratch_shapes=scratch,
        input_output_aliases=aliases or {},
        compiler_params=pltpu.CompilerParams(vmem_limit_bytes=grant * 2**20),
        cost_estimate=pl.CostEstimate(flops=int(us * 10**9) + 1, bytes_accessed=int(us * 3 * 10**6) + 1, transcendentals=0),
    )(*(x for x, _ in ins))


def place(extent_ref):
    pos = lax.axis_index("sub")
    top = lax.axis_size("sub").bit_length() - 2
    core = pos & 1
    side = (pos >> top) & 1
    even = pos - core
    return core, side, extent_ref[even], extent_ref[even ^ (1 << top)]


def wait_whole(ref, sem):
    pltpu.make_async_copy(ref, ref, sem).wait()


def run_copies(copies, sems):
    handles = [pltpu.make_async_copy(src, dst, sems.at[i]) for i, (src, dst) in enumerate(copies)]
    for handle in handles:
        handle.start()
    for handle in handles:
        handle.wait()


def load_rows(images_ref, field_ref, side, sems):
    loads = []
    for part in range(2):
        rows = pl.ds(pl.multiple_of(part * ROW + side * QRT, QRT), QRT)
        source = images_ref.at[:, rows, pl.ds(0, field_ref.shape[-1])]
        loads.append(pltpu.make_async_copy(source, field_ref.at[part], sems.at[part]))
        loads[-1].start()
    return loads


def read_block(field_ref, part, block):
    return field_ref[part, :, :, pl.ds(pl.multiple_of(block * BLK, BLK), BLK)]


def slot_block(extent, slot):
    part = (slot >= extent).astype(jnp.int32)
    return part, slot - part * extent


def halo_blocks(sz, extent, first):
    part, block = slot_block(extent, first)
    left = (part, jnp.maximum(block - 1, 0))
    part, block = slot_block(extent, first + sz.slots - 1)
    return left, (part, block + 1), (0, extent)


def load_parameters(shift_ref, taps_ref, phase_ref, raw_ref, pieces_ref, angles_ref, sems):
    pairs = [(shift_ref, raw_ref), (taps_ref, pieces_ref), (phase_ref, angles_ref)]
    loads = [pltpu.make_async_copy(*pair, sems.at[i]) for i, pair in enumerate(pairs)]
    for load in loads:
        load.start()
    return loads


def turn_parameters(sz, levels, raw_ref, pieces_ref, angles_ref, moved_ref, turned_ref, shifts_ref):
    half = BLK // 2
    for l in levels:
        moved_ref[...] = jnp.zeros((BLK, BLK), F32)
        for s in range(2):
            at = BASE[s] + sz.used
            moved_ref[at : at + 4, 0:half] = pieces_ref[l, s]
            moved_ref[at + 4 : at + 6, 0:half] = angles_ref[l, s]
            shifts_ref[l, s] = jnp.zeros((half, BLK), F32)
            shifts_ref[l, s, :, 0:half] = raw_ref[l, s].astype(F32)
        turned_ref[l] = moved_ref[...].T[0:half]


def window_parameters(sz, turned_ref, shifts_ref, l, row, first, extent, core):
    lane = lax.broadcasted_iota(jnp.int32, (ROW, BLK), 1)
    rows = pl.ds(pl.multiple_of(row, ROW), ROW)
    result = turned_ref[l, rows, :]
    for s in range(2):
        shifts = shifts_ref[l, s, rows, :]
        at = BASE[s]
        turn = lambda by: pltpu.roll(shifts, jnp.bitwise_and(by, BLK - 1), 1)
        inside = jnp.logical_and(lane >= at, lane < at + sz.middle)
        result = jnp.where(inside, turn(at + 1 - first + core * extent), result)
        result = jnp.where(lane == at + sz.middle, turn(at + sz.middle - extent), result)
    return result


def head_body(sz, extent_ref, images_ref, shift_ref, taps_ref, phase_ref, same_ref, cross_ref,
              mate_par, own_par,
              piece_ref, edge_ref, moved_ref, turned_ref, shifts_ref, raw_ref, pieces_ref, angles_ref,
              sems, par_sems):
    core, side, own, other = place(extent_ref)
    windows = (core * sz.slots, (1 - core) * sz.slots)
    small = load_parameters(shift_ref, taps_ref, phase_ref, raw_ref, pieces_ref, angles_ref, par_sems)
    count = piece_ref.shape[1] - 1

    def fetch(part, block, dst, sem):
        rows = pl.ds(pl.multiple_of(part * ROW + (1 - side) * QRT, QRT), QRT)
        lanes = pl.ds(pl.multiple_of(block * BLK, BLK), BLK)
        pltpu.make_async_copy(images_ref.at[:, rows, lanes], dst, sem).start()

    for i in range(2):
        for n, (part, block) in enumerate(halo_blocks(sz, other, windows[i])):
            fetch(part, block, edge_ref.at[i, n], sems.at[0])
    for i in range(2):
        for j in range(count):
            fetch(*slot_block(other, windows[i] + j), piece_ref.at[i, j], sems.at[1])
    for load in small:
        load.wait()
    turn_parameters(sz, (0,), raw_ref, pieces_ref, angles_ref, moved_ref, turned_ref, shifts_ref)
    lane = lax.broadcasted_iota(jnp.int32, (ROW, BLK), 1)
    results = [
        window_parameters(sz, turned_ref, shifts_ref, 0, (1 - side) * ROW, windows[i], other, core)
        for i in range(2)
    ]
    wait_whole(edge_ref, sems.at[0])
    for i in range(2):
        left, right, middle = (edge_ref[i, n].reshape(ROW, BLK) for n in range(3))
        result = jnp.where(lane < 2 * REACH, pltpu.roll(middle, REACH, 1), results[i])
        result = jnp.where(lane < REACH, right, result)
        result = jnp.where(lane >= BLK - 2, left, result)
        piece_ref[i, count] = result.reshape(2, QRT, BLK)
    wait_whole(piece_ref.at[:, pl.ds(0, count)], sems.at[1])
    stores = [(piece_ref.at[0], same_ref), (piece_ref.at[1], cross_ref)]
    stores = [pltpu.make_async_copy(*pair, sems.at[i]) for i, pair in enumerate(stores)]
    for store in stores:
        store.start()
    turn_parameters(sz, (1,), raw_ref, pieces_ref, angles_ref, moved_ref, turned_ref, shifts_ref)
    for i, level, row in ((0, 0, side * ROW), (1, 1, 0), (2, 1, ROW)):
        made = [
            window_parameters(sz, turned_ref, shifts_ref, level, row, first, own, core)
            for first in windows
        ]
        own_par[i] = made[0]
        mate_par[i] = made[1].reshape(2, QRT, BLK)
    for store in stores:
        store.wait()


def near_body(sz, chunks, pieces, extent_ref, images_ref, par_ref, *rest):
    *rest, far_ref, field_ref, far_sems, sems, out_sems = rest
    sends = 2 * len(chunks) - 2
    homes, outs = rest[: len(rest) // 2], rest[len(rest) // 2 :]
    mates, kept = outs[sends:-1], outs[-1]
    core, side, own, other = place(extent_ref)
    windows = (core * sz.slots, (1 - core) * sz.slots)
    far_loads = load_rows(images_ref, far_ref, 1 - side, far_sems)
    loads = load_rows(images_ref, field_ref, side, sems)
    length = mates[0].shape[0]
    last_load = pltpu.make_async_copy(par_ref, mates[-1].at[pl.ds(length - 3, 3)], sems.at[2])
    last_load.start()
    stores = [pltpu.make_async_copy(outs[i], homes[i], out_sems.at[i]) for i in range(len(outs))]
    for load in far_loads:
        load.wait()
    begin = chunks[0]
    for k, count in enumerate(chunks[1:]):
        for i in range(2):
            for j in range(count):
                where = slot_block(other, windows[i] + begin + j)
                outs[2 * k + i][j] = read_block(far_ref, *where)
            stores[2 * k + i].start()
        begin += count
    for load in loads:
        load.wait()

    def put(first, where):
        for x, at in zip((0, sz.right, sz.middle), halo_blocks(sz, own, first)):
            where(x, read_block(field_ref, *at))
        for j in range(sz.slots):
            where(1 + j, read_block(field_ref, *slot_block(own, first + j)))

    def mate_at(x, value):
        mates[x // length][x % length] = value

    def kept_at(x, value):
        kept[x] = value

    put(windows[1], mate_at)
    last_load.wait()
    for store in stores[sends:-1]:
        store.start()
    put(windows[0], kept_at)
    stores[-1].start()
    for store in stores:
        store.wait()


def build_tables(sz, par_ref, tab_ref, ltab_ref, groups, extent, first):
    lane = lax.broadcasted_iota(jnp.int32, (QRT, BLK), 1)
    middle = lane == sz.middle
    even = jnp.logical_or(first + lane - 1 < extent, middle)
    block = jnp.where(even, first - 1 + lane, first - 1 + lane - extent)
    block = jnp.where(middle, extent, block).astype(F32)
    for group in range(groups):
        rows = [par_ref[p, pl.ds(group, QRT, stride=groups), :] for p in range(2)]
        for s in range(2):

            def spread(p, n):
                c = BASE[s] + sz.used + n
                return jnp.broadcast_to(rows[p][:, c : c + 1], (QRT, BLK))

            column = lambda n: jnp.where(even, spread(0, n), spread(1, n))
            tab_ref[s, group, 0] = jnp.where(
                even,
                pltpu.roll(rows[0], BLK - BASE[s], 1),
                pltpu.roll(rows[1], BLK - BASE[s], 1),
            )
            angle = column(4) + column(5) * (block * (BLK / sz.total))
            tab_ref[s, group, 1] = jnp.cos(angle)
            tab_ref[s, group, 2] = jnp.sin(angle)
            for p in range(2):
                angle = spread(p, 5) * (lane.astype(F32) / sz.total)
                ltab_ref[p, s, group, 0] = jnp.cos(angle)
                ltab_ref[p, s, group, 1] = jnp.sin(angle)
                for k in range(4):
                    ltab_ref[p, s, group, 2 + k] = spread(p, k)


def gathered(tab_ref, ltab_ref, s, group, x, part, rows):
    pick = jnp.full((8, BLK), x, jnp.int32)
    shift, cb, sb = (
        jnp.take_along_axis(tab_ref[s, group, k, rows, :], pick, axis=1) for k in range(3)
    )
    cl, sl, *taps = (ltab_ref[part, s, group, k, rows, :] for k in range(6))
    two = shift > 1.5
    one = jnp.where(two, shift - 2.0, shift) > 0.5
    zero = jnp.zeros((8, BLK), F32)
    taps = [zero] + taps + [zero]
    taps = [zero] * 2 + [jnp.where(one, taps[k], taps[k + 1]) for k in range(5)] + [zero] * 2
    weights = [jnp.where(two, taps[k], taps[k + 2]) for k in range(7)]
    return weights + [cb * cl - sb * sl, sb * cl + cb * sl]


def merge_block(sources, load, coef, sums, x, before, after, store):
    lane = lax.broadcasted_iota(jnp.int32, (8, BLK), 1)
    for s in sources:
        moved = []
        for ri in range(2):
            cur, prv, nxt = load(s, x, ri), load(s, before, ri), load(s, after, ri)
            views = [pltpu.roll(jnp.where(lane == BLK - 1, prv, cur), 1, 1), cur]
            for o in range(1, 6):
                views.append(pltpu.roll(jnp.where(lane < o, nxt, cur), BLK - o, 1))
            moved.append(views)
        for u in range(2):
            *weights, cosine, sine = coef(s, u)
            value = []
            for ri in range(2):
                total = weights[0] * moved[ri][0]
                for k in range(1, 7):
                    total = total + weights[k] * moved[ri][k]
                value.append(total)
            real = cosine * value[0] - sine * value[1]
            imag = sine * value[0] + cosine * value[1]
            sums[u] = [real, imag] if sums[u] is None else [sums[u][0] + real, sums[u][1] + imag]
    for u in range(2):
        for ri in range(2):
            store(u, ri, sums[u][ri])


def level_one(d_ref, f_ref, coef, x, before, after):
    for h in range(2):
        rows = lambda ri: pl.ds(QRT * ri + 8 * h, 8)

        def store(u, ri, value):
            f_ref[x, u, rows(ri), :] = value

        merge_block(
            (0, 1), lambda s, at, ri: d_ref[s, at, rows(ri), :],
            lambda s, u: coef(pl.ds(8 * h, 8), s, u), [None, None], x, before, after, store,
        )


def level_two(f_ref, coef, start, store, x, before, after):
    for u1 in range(2):
        for h in range(2):
            sums = [start(2 * u1 + u, h) for u in range(2)]
            merge_block(
                (0,), lambda s, at, ri: f_ref[at, u1, pl.ds(QRT * ri + 8 * h, 8), :],
                lambda s, u: coef(pl.ds(8 * h, 8), 2 * u1 + u), sums, x, before, after,
                lambda u, ri, value: store(2 * u1 + u, h, ri, value),
            )


def neighbours(sz, slot, first, extent):
    where = first + slot
    before = jnp.where(jnp.logical_or(where == 0, where == extent), sz.zero, slot)
    after = jnp.where(where == extent - 1, sz.middle, slot + 2)
    return before, after, (where >= extent).astype(jnp.int32)


def loop(begin, end, body):
    def step(slot, carry):
        body(slot)
        return carry

    lax.fori_loop(begin, end, step, 0, unroll=4)


def level_one_all(sz, d_ref, f_ref, coef_at, slots, left, right, low, high, first, extent):
    part_of = lambda slot: (first + slot >= extent).astype(jnp.int32)

    def body(slot):
        before, after, part = neighbours(sz, slot, first, extent)
        level_one(d_ref, f_ref, coef_at(slot + 1, part), slot + 1, before, after)

    if left:
        level_one(d_ref, f_ref, coef_at(0, part_of(0)), 0, 0, 1)
    loop(*slots, body)
    if right:
        part = part_of(sz.slots - 1)
        level_one(d_ref, f_ref, coef_at(sz.right, part), sz.right, sz.slots, sz.zero)
    before = jnp.clip(extent - first, low + 1, high)
    level_one(d_ref, f_ref, coef_at(sz.middle, 0), sz.middle, before, sz.zero)


def table_coef(tab, ltab):
    return lambda x, part: (lambda rows, s, u: gathered(tab, ltab, s, u, x, part, rows))


def local_body(sz, pieces, extent_ref, kept, par, *rest):
    mates = rest[:pieces]
    (share_out, tab2_out, ltab2_out, d, f, par1s, par2s, tab, ltab, tab2, ltab2, share,
     sems, out_sems) = rest[pieces:]
    core, side, extent, _ = place(extent_ref)
    first = core * sz.slots
    used = sz.used
    copies = [
        (kept, d.at[core, pl.ds(0, used)]),
        (par.at[0], par1s.at[core]),
        (par.at[1], par2s.at[core, pl.ds(0, ROW)]),
        (par.at[2], par2s.at[core, pl.ds(ROW, ROW)]),
    ]
    length = mates[0].shape[0]
    for i, mate in enumerate(mates):
        count = min(length, used - i * length)
        copies.append((mate.at[pl.ds(0, count)], d.at[1 - core, pl.ds(i * length, count)]))
    copies += [
        (mates[-1].at[length - 3], par1s.at[1 - core]),
        (mates[-1].at[length - 2], par2s.at[1 - core, pl.ds(0, ROW)]),
        (mates[-1].at[length - 1], par2s.at[1 - core, pl.ds(ROW, ROW)]),
    ]
    run_copies(copies, sems)
    zeros = jnp.zeros((ROW, BLK), F32)
    for s in range(2):
        d[s, sz.zero] = zeros
        f[sz.zero, s] = zeros
    build_tables(sz, par1s, tab, ltab, 2, extent, first)
    build_tables(sz, par2s, tab2, ltab2, 4, extent, first)
    level_one_all(
        sz, d, f, table_coef(tab, ltab), (0, sz.slots), True, True, 0, sz.slots, first, extent
    )
    def body(slot):
        before, after, part = neighbours(sz, slot, first, extent)

        def store(u, h, ri, value):
            share[slot, ri, u, pl.ds(8 * h, 8), :] = value

        level_two(
            f, lambda rows, u: gathered(tab2, ltab2, side, u, slot + 1, part, rows),
            lambda u, h: None, store, slot + 1, before, after,
        )

    loop(0, sz.slots, body)
    run_copies([(share, share_out), (tab2, tab2_out), (ltab2, ltab2_out)], out_sems)


def one_range(sz, begin, count):
    end = begin + count
    return (0 if begin == 0 else begin - 1), (end if end == sz.slots else end - 1)


def two_range(sz, begin, count):
    end = begin + count
    return (0 if begin == 0 else begin - 2), (end if end == sz.slots else end - 2)


def other_tables_body(sz, spans, extent_ref, halo_same, halo_cross, tab2, ltab2, tab, ltab, *rest):
    wides, pars = rest[:-1], rest[-1]
    core, side, extent, _ = place(extent_ref)
    first = core * sz.slots
    pars[core] = halo_same[halo_same.shape[0] - 1]
    pars[1 - core] = halo_cross[halo_cross.shape[0] - 1]
    build_tables(sz, pars, tab, ltab, 2, extent, first)
    rows = lambda h: pl.ds(8 * h, 8)
    for n, span in enumerate(spans):
        wide1, wide2 = wides[2 * n : 2 * n + 2]
        one, two = one_range(sz, *span), two_range(sz, *span)

        def spread_one(j, x, part):
            for s in range(2):
                for u in range(2):
                    for h in range(2):
                        values = gathered(tab, ltab, s, u, x, part, rows(h))
                        for k, value in enumerate(values):
                            wide1[j, s, u, k, rows(h), :] = value

        def body_one(slot):
            _, _, part = neighbours(sz, slot, first, extent)
            spread_one(slot - one[0], slot + 1, part)

        def body_two(slot):
            _, _, part = neighbours(sz, slot, first, extent)
            for u in range(4):
                for h in range(2):
                    values = gathered(tab2, ltab2, 1 - side, u, slot + 1, part, rows(h))
                    for k, value in enumerate(values):
                        wide2[slot - two[0], u, k, rows(h), :] = value

        loop(*one, body_one)
        _, _, part = neighbours(sz, sz.slots - 1, first, extent)
        count = one[1] - one[0]
        spread_one(count, sz.middle, 0)
        if one[1] == sz.slots:
            spread_one(count + 1, sz.right, part)
        loop(*two, body_two)


def gate_body(*refs):
    pass


def main_body(sz, begin, count, wide, extent_ref, *rest):
    head, last = begin == 0, begin + count == sz.slots
    ins = list(rest)

    def take(n):
        part = ins[:n]
        del ins[:n]
        return part

    same, cross, halo_same, halo_cross, share = take(5)
    tables = take(2 if wide else 4)
    if not head:
        dtail_in, ftail_in, _ = take(3)
    (out,) = take(1)
    if not last:
        dtail_out, ftail_out = take(2)
    d, f, o, out_sem = ins
    core, side, extent, _ = place(extent_ref)
    first = core * sz.slots
    end = begin + count
    low = 0 if head else begin - 2
    zeros = jnp.zeros((ROW, BLK), F32)
    for mine, chunk, halo in ((core, same, halo_same), (1 - core, cross, halo_cross)):
        for i in range(count):
            d[mine, begin + 1 + i] = chunk[i]
        edge = halo[halo.shape[0] - 1]
        if head:
            d[mine, 0] = edge
        if last:
            d[mine, sz.right] = edge
        d[mine, sz.middle] = pltpu.roll(edge, BLK - REACH, 1)
    for s in range(2):
        d[s, sz.zero] = zeros
        f[sz.zero, s] = zeros
        if not head:
            for i in range(2):
                d[s, begin - 1 + i] = dtail_in[s, i]
                f[begin - 2 + i, s] = ftail_in[i, s]

    slots = one_range(sz, begin, count)
    if wide:
        wide1, wide2 = tables

        def coef_at(x, part):
            if isinstance(x, int):
                j = slots[1] - slots[0] + (1 if x == sz.right else 0)
            else:
                j = x - 1 - slots[0]
            return lambda rows, s, u: [wide1[j, s, u, k, rows, :] for k in range(9)]
    else:
        tab1, ltab1, tab2, ltab2 = tables
        coef_at = table_coef(tab1, ltab1)
    level_one_all(sz, d, f, coef_at, slots, head, last, low, end, first, extent)

    def body(slot):
        before, after, part = neighbours(sz, slot, first, extent)
        at = slot - low

        def store(u, h, ri, value):
            o[at, ri, pl.ds(32 * h + u, 8, stride=4), :] = value

        if wide:
            coef = lambda rows, u: [wide2[at, u, k, rows, :] for k in range(9)]
        else:
            coef = lambda rows, u: gathered(tab2, ltab2, 1 - side, u, slot + 1, part, rows)
        level_two(
            f, coef, lambda u, h: [share[slot, ri, u, pl.ds(8 * h, 8), :] for ri in range(2)],
            store, slot + 1, before, after,
        )
        lanes = pl.ds(pl.multiple_of(slot * BLK, BLK), BLK)
        pltpu.make_async_copy(o.at[at], out.at[:, :, lanes], out_sem).start()

    loop(*two_range(sz, begin, count), body)
    if not last:
        for s in range(2):
            for i in range(2):
                dtail_out[s, i] = d[s, end - 1 + i]
                ftail_out[i, s] = f[end - 2 + i, s]
    wait_whole(o, out_sem)


def per_device(images, band_shift, tap_weights, phases, extent_map):
    total_rows = images.shape[2]
    beams = images.shape[1]
    slots = total_rows // BLK // 2
    sz = Sizes(slots, total_rows)
    chunks = CHUNKS
    assert beams == 4 * QRT and sum(chunks) == slots and len(chunks) > 2
    assert sz.used + 6 <= BASE[1] - BASE[0] and BASE[1] + sz.used + 6 <= BLK - 2
    size = lax.axis_size("sub")
    top = 1 << (size.bit_length() - 2)
    swap = lambda x, by: lax.ppermute(x, "sub", [(i, i ^ by) for i in range(size)])
    flat = lambda x: x.reshape(x.shape[0], ROW, BLK)
    extents = (extent_map, SMEM)
    vm = lambda *dims: VMEM(dims, F32)

    half = BLK // 2
    blocks = lambda n: (shape(n, 2, QRT, BLK), ANY)
    lanes = (3 * slots // 2 + 1) * BLK
    count = chunks[0] + 1
    *first, mate_par, own_par = call(
        functools.partial(head_body, sz),
        [
            extents,
            (images, HBM),
            (band_shift[0], HBM),
            (tap_weights[0].transpose(0, 1, 3, 2), HBM),
            (phases[0].transpose(0, 1, 3, 2), HBM),
        ],
        [blocks(count)] * 2 + [(shape(3, 2, QRT, BLK), VMEM), (shape(3, ROW, BLK), VMEM)],
        [vm(2, count, 2, QRT, BLK), vm(2, 3, 2, QRT, BLK), vm(BLK, BLK), vm(2, half, BLK),
         vm(2, 2, half, BLK), VMEM((2, 2, half, half), jnp.int32), vm(2, 2, 4, half),
         vm(2, 2, 2, half), DMA((2,)), DMA((3,))],
        grant=56,
    )
    length = -(-(sz.used + 3) // MATES)
    counts = [n for n in chunks[1:] for _ in range(2)] + [length] * MATES + [sz.used]
    *packed, kept = call(
        functools.partial(near_body, sz, chunks, MATES),
        [extents, (images, HBM), (mate_par, ANY)], [blocks(n) for n in counts],
        [vm(n, 2, QRT, BLK) for n in counts] + [vm(2, 2, QRT, lanes)] * 2
        + [DMA((2,)), DMA((3,)), DMA((len(counts),))],
        grant=56,
    )
    packed, mates = list(first) + packed[:-MATES], packed[-MATES:]
    mates, kept = [flat(swap(x, 1)) for x in mates], flat(kept)
    send = lambda a, b: (flat(swap(a, top)), flat(swap(b, top ^ 1)))
    def gate(waiting, needed):
        passed = [(x, ANY) for x in waiting]
        out = call(gate_body, passed + [(x, ANY) for x in needed], passed, [], {0: 0, 1: 1})
        return send(*out)

    got = [send(*packed[0:2])]
    got.append(gate(packed[2:4], mates) if GATED else send(*packed[2:4]))
    halo = [(x, VMEM) for x in got[0]]

    tabs1, ltabs1 = (2, 2, 3, QRT, BLK), (2, 2, 2, 6, QRT, BLK)
    tabs2, ltabs2 = (2, 4, 3, QRT, BLK), (2, 2, 4, 6, QRT, BLK)
    shares = (slots, 2, 4, QRT, BLK)
    d_s, f_s = (2, sz.zero + 1, ROW, BLK), (sz.zero + 1, 2, ROW, BLK)
    share, tab2, ltab2 = call(
        functools.partial(local_body, sz, MATES),
        [extents, (kept, HBM), (own_par, HBM)] + [(x, HBM) for x in mates],
        [(shape(*shares), ANY), (shape(*tabs2), ANY), (shape(*ltabs2), ANY)],
        [vm(*d_s), vm(*f_s), vm(2, ROW, BLK), vm(2, 2 * ROW, BLK), vm(*tabs1), vm(*ltabs1),
         vm(*tabs2), vm(*ltabs2), vm(*shares), DMA((7 + MATES,)), DMA((3,))],
        us=LOCAL,
    )

    begins = [sum(chunks[:k]) for k in range(len(chunks))]
    spans = [(begins[k], chunks[k]) for k in range(WIDE, len(chunks))]
    outs = [tabs1, ltabs1]
    for span in spans:
        one, two = one_range(sz, *span), two_range(sz, *span)
        extra = 2 if one[1] == slots else 1
        outs += [(one[1] - one[0] + extra, 2, 2, 9, QRT, BLK), (two[1] - two[0], 4, 9, QRT, BLK)]
    got.append(gate(packed[4:6], [*got[0], share]))
    tab1, ltab1, *wides = call(
        functools.partial(other_tables_body, sz, spans),
        [extents, *halo, (tab2, VMEM), (ltab2, VMEM)],
        [(shape(*s), VMEM) for s in outs], [vm(2, ROW, BLK)], us=HINT,
    )
    tail = [(shape(2, 2, ROW, BLK), VMEM)] * 2
    out = None
    for k, count in enumerate(chunks):
        begin = begins[k]
        head, last = k == 0, k == len(chunks) - 1
        if k >= 1 and k + 2 < len(chunks):
            got.append(gate(packed[2 * k + 4 : 2 * k + 6], [*got[k], dtail]))
        ins = [extents, *((x, VMEM) for x in got[k]), *halo, (share, VMEM)]
        if k >= WIDE:
            ins += [(x, VMEM) for x in wides[2 * (k - WIDE) : 2 * (k - WIDE) + 2]]
        else:
            ins += [(x, VMEM) for x in (tab1, ltab1, tab2, ltab2)]
        outs = [(shape(2, beams, slots * BLK), HBM)]
        aliases = {}
        if not head:
            aliases[len(ins) + 2] = 0
            ins += [(dtail, VMEM), (ftail, VMEM), (out, HBM)]
        if not last:
            outs += tail
        low, top_slot = two_range(sz, begin, count)
        res = call(
            functools.partial(main_body, sz, begin, count, k >= WIDE), ins, outs,
            [vm(*d_s), vm(*f_s), vm(top_slot - low, 2, beams, BLK), DMA], aliases, us=HINT if head else 0.1,
        )
        out = res[0]
        if not last:
            dtail, ftail = res[1:]
    return out


def solution(mesh):
    placed = (
        P(None, None, ("strip", "sub")),
        P(("strip", "sub"), None, None, None, None),
        P(("strip", "sub"), None, None, None, None),
        P(("strip", "sub"), None, None, None, None),
        P("strip"),
    )
    return jax.shard_map(
        per_device,
        mesh=mesh,
        in_specs=placed,
        out_specs=P(None, None, ("strip", "sub")),
        check_vma=False,
    )
```

```python
import functools

import jax
import jax.numpy as jnp
from jax import lax
from jax.experimental import pallas as pl
from jax.experimental.pallas import tpu as pltpu
from jax.sharding import PartitionSpec as P

BLK = 128
QRT = 16
ROW = 2 * QRT
CHUNKS = (18, 9, 5)
HINT = 0
LOCAL = 0
MATES = 3
GATED = True
WIDE = 2

REACH = 10
BASE = (24, 72)


class Sizes:
    def __init__(self, slots, total_rows):
        self.slots = slots
        self.total = total_rows
        self.right = slots + 1
        self.middle = slots + 2
        self.zero = slots + 3
        self.used = slots + 3


F32 = jnp.float32
ANY, HBM, VMEM, SMEM = pl.ANY, pltpu.HBM, pltpu.VMEM, pltpu.SMEM
DMA = pltpu.SemaphoreType.DMA


def shape(*dims):
    return jax.ShapeDtypeStruct(dims, F32)


def call(body, ins, outs, scratch, aliases=None, grant=32, us=0):
    return pl.pallas_call(
        body,
        out_shape=tuple(x for x, _ in outs),
        in_specs=[pl.BlockSpec(memory_space=m) for _, m in ins],
        out_specs=tuple(pl.BlockSpec(memory_space=m) for _, m in outs),
        scratch_shapes=scratch,
        input_output_aliases=aliases or {},
        compiler_params=pltpu.CompilerParams(vmem_limit_bytes=grant * 2**20),
        cost_estimate=pl.CostEstimate(flops=int(us * 10**9) + 1, bytes_accessed=int(us * 3 * 10**6) + 1, transcendentals=0),
    )(*(x for x, _ in ins))


def place(extent_ref):
    pos = lax.axis_index("sub")
    top = lax.axis_size("sub").bit_length() - 2
    core = pos & 1
    side = (pos >> top) & 1
    even = pos - core
    return core, side, extent_ref[even], extent_ref[even ^ (1 << top)]


def wait_whole(ref, sem):
    pltpu.make_async_copy(ref, ref, sem).wait()


def run_copies(copies, sems):
    handles = [pltpu.make_async_copy(src, dst, sems.at[i]) for i, (src, dst) in enumerate(copies)]
    for handle in handles:
        handle.start()
    for handle in handles:
        handle.wait()


def load_rows(images_ref, field_ref, side, sems):
    loads = []
    for part in range(2):
        rows = pl.ds(pl.multiple_of(part * ROW + side * QRT, QRT), QRT)
        source = images_ref.at[:, rows, pl.ds(0, field_ref.shape[-1])]
        loads.append(pltpu.make_async_copy(source, field_ref.at[part], sems.at[part]))
        loads[-1].start()
    return loads


def read_block(field_ref, part, block):
    return field_ref[part, :, :, pl.ds(pl.multiple_of(block * BLK, BLK), BLK)]


def slot_block(extent, slot):
    part = (slot >= extent).astype(jnp.int32)
    return part, slot - part * extent


def halo_blocks(sz, extent, first):
    part, block = slot_block(extent, first)
    left = (part, jnp.maximum(block - 1, 0))
    part, block = slot_block(extent, first + sz.slots - 1)
    return left, (part, block + 1), (0, extent)


def load_parameters(shift_ref, taps_ref, phase_ref, raw_ref, pieces_ref, angles_ref, sems):
    pairs = [(shift_ref, raw_ref), (taps_ref, pieces_ref), (phase_ref, angles_ref)]
    loads = [pltpu.make_async_copy(*pair, sems.at[i]) for i, pair in enumerate(pairs)]
    for load in loads:
        load.start()
    return loads


def turn_parameters(sz, levels, raw_ref, pieces_ref, angles_ref, moved_ref, turned_ref, shifts_ref):
    half = BLK // 2
    for l in levels:
        moved_ref[...] = jnp.zeros((BLK, BLK), F32)
        for s in range(2):
            at = BASE[s] + sz.used
            moved_ref[at : at + 4, 0:half] = pieces_ref[l, s]
            moved_ref[at + 4 : at + 6, 0:half] = angles_ref[l, s]
            shifts_ref[l, s] = jnp.zeros((half, BLK), F32)
            shifts_ref[l, s, :, 0:half] = raw_ref[l, s].astype(F32)
        turned_ref[l] = moved_ref[...].T[0:half]


def window_parameters(sz, turned_ref, shifts_ref, l, row, first, extent, core):
    lane = lax.broadcasted_iota(jnp.int32, (ROW, BLK), 1)
    rows = pl.ds(pl.multiple_of(row, ROW), ROW)
    result = turned_ref[l, rows, :]
    for s in range(2):
        shifts = shifts_ref[l, s, rows, :]
        at = BASE[s]
        turn = lambda by: pltpu.roll(shifts, jnp.bitwise_and(by, BLK - 1), 1)
        inside = jnp.logical_and(lane >= at, lane < at + sz.middle)
        result = jnp.where(inside, turn(at + 1 - first + core * extent), result)
        result = jnp.where(lane == at + sz.middle, turn(at + sz.middle - extent), result)
    return result


def head_body(sz, extent_ref, images_ref, shift_ref, taps_ref, phase_ref, same_ref, cross_ref,
              piece_ref, edge_ref, moved_ref, turned_ref, shifts_ref, raw_ref, pieces_ref, angles_ref,
              sems, par_sems):
    core, side, _, other = place(extent_ref)
    windows = (core * sz.slots, (1 - core) * sz.slots)
    small = load_parameters(shift_ref, taps_ref, phase_ref, raw_ref, pieces_ref, angles_ref, par_sems)
    count = piece_ref.shape[1] - 1

    def fetch(part, block, dst, sem):
        rows = pl.ds(pl.multiple_of(part * ROW + (1 - side) * QRT, QRT), QRT)
        lanes = pl.ds(pl.multiple_of(block * BLK, BLK), BLK)
        pltpu.make_async_copy(images_ref.at[:, rows, lanes], dst, sem).start()

    for i in range(2):
        for n, (part, block) in enumerate(halo_blocks(sz, other, windows[i])):
            fetch(part, block, edge_ref.at[i, n], sems.at[0])
    for i in range(2):
        for j in range(count):
            fetch(*slot_block(other, windows[i] + j), piece_ref.at[i, j], sems.at[1])
    for load in small:
        load.wait()
    turn_parameters(sz, (0,), raw_ref, pieces_ref, angles_ref, moved_ref, turned_ref, shifts_ref)
    lane = lax.broadcasted_iota(jnp.int32, (ROW, BLK), 1)
    results = [
        window_parameters(sz, turned_ref, shifts_ref, 0, (1 - side) * ROW, windows[i], other, core)
        for i in range(2)
    ]
    wait_whole(edge_ref, sems.at[0])
    for i in range(2):
        left, right, middle = (edge_ref[i, n].reshape(ROW, BLK) for n in range(3))
        result = jnp.where(lane < 2 * REACH, pltpu.roll(middle, REACH, 1), results[i])
        result = jnp.where(lane < REACH, right, result)
        result = jnp.where(lane >= BLK - 2, left, result)
        piece_ref[i, count] = result.reshape(2, QRT, BLK)
    wait_whole(piece_ref.at[:, pl.ds(0, count)], sems.at[1])
    stores = [(piece_ref.at[0], same_ref), (piece_ref.at[1], cross_ref)]
    stores = [pltpu.make_async_copy(*pair, sems.at[i]) for i, pair in enumerate(stores)]
    for store in stores:
        store.start()
    for store in stores:
        store.wait()


def near_body(sz, chunks, extent_ref, images_ref, shift_ref, taps_ref, phase_ref, _, *rest):
    (*rest, far_ref, field_ref, moved_ref, turned_ref, shifts_ref, raw_ref, pieces_ref, angles_ref,
     far_sems, sems, par_sems, out_sems) = rest
    sends = 2 * len(chunks) - 2
    total = (len(rest) - 1) // 2
    homes, own_par, outs = rest[:total], rest[total], rest[total + 1 :]
    mates, kept = outs[sends:-1], outs[-1]
    core, side, own, other = place(extent_ref)
    windows = (core * sz.slots, (1 - core) * sz.slots)
    far_loads = load_rows(images_ref, far_ref, 1 - side, far_sems)
    loads = load_rows(images_ref, field_ref, side, sems)
    length = mates[0].shape[0]
    small = load_parameters(shift_ref, taps_ref, phase_ref, raw_ref, pieces_ref, angles_ref, par_sems)
    stores = [pltpu.make_async_copy(outs[i], homes[i], out_sems.at[i]) for i in range(len(outs))]
    for load in far_loads:
        load.wait()
    begin = chunks[0]
    for k, count in enumerate(chunks[1:]):
        for i in range(2):
            for j in range(count):
                where = slot_block(other, windows[i] + begin + j)
                outs[2 * k + i][j] = read_block(far_ref, *where)
            stores[2 * k + i].start()
        begin += count
    for load in small:
        load.wait()
    turn_parameters(sz, (0, 1), raw_ref, pieces_ref, angles_ref, moved_ref, turned_ref, shifts_ref)
    for i, level, row in ((0, 0, side * ROW), (1, 1, 0), (2, 1, ROW)):
        made = [
            window_parameters(sz, turned_ref, shifts_ref, level, row, first, own, core)
            for first in windows
        ]
        own_par[i] = made[0]
        mates[-1][length - 3 + i] = made[1].reshape(2, QRT, BLK)
    for load in loads:
        load.wait()

    def put(first, where):
        for x, at in zip((0, sz.right, sz.middle), halo_blocks(sz, own, first)):
            where(x, read_block(field_ref, *at))
        for j in range(sz.slots):
            where(1 + j, read_block(field_ref, *slot_block(own, first + j)))

    def mate_at(x, value):
        mates[x // length][x % length] = value

    def kept_at(x, value):
        kept[x] = value

    put(windows[1], mate_at)
    for store in stores[sends:-1]:
        store.start()
    put(windows[0], kept_at)
    stores[-1].start()
    for store in stores:
        store.wait()


def build_tables(sz, par_ref, tab_ref, ltab_ref, groups, extent, first):
    lane = lax.broadcasted_iota(jnp.int32, (QRT, BLK), 1)
    middle = lane == sz.middle
    even = jnp.logical_or(first + lane - 1 < extent, middle)
    block = jnp.where(even, first - 1 + lane, first - 1 + lane - extent)
    block = jnp.where(middle, extent, block).astype(F32)
    for group in range(groups):
        rows = [par_ref[p, pl.ds(group, QRT, stride=groups), :] for p in range(2)]
        for s in range(2):

            def spread(p, n):
                c = BASE[s] + sz.used + n
                return jnp.broadcast_to(rows[p][:, c : c + 1], (QRT, BLK))

            column = lambda n: jnp.where(even, spread(0, n), spread(1, n))
            tab_ref[s, group, 0] = jnp.where(
                even,
                pltpu.roll(rows[0], BLK - BASE[s], 1),
                pltpu.roll(rows[1], BLK - BASE[s], 1),
            )
            angle = column(4) + column(5) * (block * (BLK / sz.total))
            tab_ref[s, group, 1] = jnp.cos(angle)
            tab_ref[s, group, 2] = jnp.sin(angle)
            for p in range(2):
                angle = spread(p, 5) * (lane.astype(F32) / sz.total)
                ltab_ref[p, s, group, 0] = jnp.cos(angle)
                ltab_ref[p, s, group, 1] = jnp.sin(angle)
                for k in range(4):
                    ltab_ref[p, s, group, 2 + k] = spread(p, k)


def gathered(tab_ref, ltab_ref, s, group, x, part, rows):
    pick = jnp.full((8, BLK), x, jnp.int32)
    shift, cb, sb = (
        jnp.take_along_axis(tab_ref[s, group, k, rows, :], pick, axis=1) for k in range(3)
    )
    cl, sl, *taps = (ltab_ref[part, s, group, k, rows, :] for k in range(6))
    two = shift > 1.5
    one = jnp.where(two, shift - 2.0, shift) > 0.5
    zero = jnp.zeros((8, BLK), F32)
    taps = [zero] + taps + [zero]
    taps = [zero] * 2 + [jnp.where(one, taps[k], taps[k + 1]) for k in range(5)] + [zero] * 2
    weights = [jnp.where(two, taps[k], taps[k + 2]) for k in range(7)]
    return weights + [cb * cl - sb * sl, sb * cl + cb * sl]


def merge_block(sources, load, coef, sums, x, before, after, store):
    lane = lax.broadcasted_iota(jnp.int32, (8, BLK), 1)
    for s in sources:
        moved = []
        for ri in range(2):
            cur, prv, nxt = load(s, x, ri), load(s, before, ri), load(s, after, ri)
            views = [pltpu.roll(jnp.where(lane == BLK - 1, prv, cur), 1, 1), cur]
            for o in range(1, 6):
                views.append(pltpu.roll(jnp.where(lane < o, nxt, cur), BLK - o, 1))
            moved.append(views)
        for u in range(2):
            *weights, cosine, sine = coef(s, u)
            value = []
            for ri in range(2):
                total = weights[0] * moved[ri][0]
                for k in range(1, 7):
                    total = total + weights[k] * moved[ri][k]
                value.append(total)
            real = cosine * value[0] - sine * value[1]
            imag = sine * value[0] + cosine * value[1]
            sums[u] = [real, imag] if sums[u] is None else [sums[u][0] + real, sums[u][1] + imag]
    for u in range(2):
        for ri in range(2):
            store(u, ri, sums[u][ri])


def level_one(d_ref, f_ref, coef, x, before, after):
    for h in range(2):
        rows = lambda ri: pl.ds(QRT * ri + 8 * h, 8)

        def store(u, ri, value):
            f_ref[x, u, rows(ri), :] = value

        merge_block(
            (0, 1), lambda s, at, ri: d_ref[s, at, rows(ri), :],
            lambda s, u: coef(pl.ds(8 * h, 8), s, u), [None, None], x, before, after, store,
        )


def level_two(f_ref, coef, start, store, x, before, after):
    for u1 in range(2):
        for h in range(2):
            sums = [start(2 * u1 + u, h) for u in range(2)]
            merge_block(
                (0,), lambda s, at, ri: f_ref[at, u1, pl.ds(QRT * ri + 8 * h, 8), :],
                lambda s, u: coef(pl.ds(8 * h, 8), 2 * u1 + u), sums, x, before, after,
                lambda u, ri, value: store(2 * u1 + u, h, ri, value),
            )


def neighbours(sz, slot, first, extent):
    where = first + slot
    before = jnp.where(jnp.logical_or(where == 0, where == extent), sz.zero, slot)
    after = jnp.where(where == extent - 1, sz.middle, slot + 2)
    return before, after, (where >= extent).astype(jnp.int32)


def loop(begin, end, body):
    def step(slot, carry):
        body(slot)
        return carry

    lax.fori_loop(begin, end, step, 0, unroll=4)


def level_one_all(sz, d_ref, f_ref, coef_at, slots, left, right, low, high, first, extent):
    part_of = lambda slot: (first + slot >= extent).astype(jnp.int32)

    def body(slot):
        before, after, part = neighbours(sz, slot, first, extent)
        level_one(d_ref, f_ref, coef_at(slot + 1, part), slot + 1, before, after)

    if left:
        level_one(d_ref, f_ref, coef_at(0, part_of(0)), 0, 0, 1)
    loop(*slots, body)
    if right:
        part = part_of(sz.slots - 1)
        level_one(d_ref, f_ref, coef_at(sz.right, part), sz.right, sz.slots, sz.zero)
    before = jnp.clip(extent - first, low + 1, high)
    level_one(d_ref, f_ref, coef_at(sz.middle, 0), sz.middle, before, sz.zero)


def table_coef(tab, ltab):
    return lambda x, part: (lambda rows, s, u: gathered(tab, ltab, s, u, x, part, rows))


def local_body(sz, pieces, extent_ref, kept, par, *rest):
    mates = rest[:pieces]
    (share_out, tab2_out, ltab2_out, d, f, par1s, par2s, tab, ltab, tab2, ltab2, share,
     sems, out_sems) = rest[pieces:]
    core, side, extent, _ = place(extent_ref)
    first = core * sz.slots
    used = sz.used
    copies = [
        (kept, d.at[core, pl.ds(0, used)]),
        (par.at[0], par1s.at[core]),
        (par.at[1], par2s.at[core, pl.ds(0, ROW)]),
        (par.at[2], par2s.at[core, pl.ds(ROW, ROW)]),
    ]
    length = mates[0].shape[0]
    for i, mate in enumerate(mates):
        count = min(length, used - i * length)
        copies.append((mate.at[pl.ds(0, count)], d.at[1 - core, pl.ds(i * length, count)]))
    copies += [
        (mates[-1].at[length - 3], par1s.at[1 - core]),
        (mates[-1].at[length - 2], par2s.at[1 - core, pl.ds(0, ROW)]),
        (mates[-1].at[length - 1], par2s.at[1 - core, pl.ds(ROW, ROW)]),
    ]
    run_copies(copies, sems)
    zeros = jnp.zeros((ROW, BLK), F32)
    for s in range(2):
        d[s, sz.zero] = zeros
        f[sz.zero, s] = zeros
    build_tables(sz, par1s, tab, ltab, 2, extent, first)
    build_tables(sz, par2s, tab2, ltab2, 4, extent, first)
    level_one_all(
        sz, d, f, table_coef(tab, ltab), (0, sz.slots), True, True, 0, sz.slots, first, extent
    )
    def body(slot):
        before, after, part = neighbours(sz, slot, first, extent)

        def store(u, h, ri, value):
            share[slot, ri, u, pl.ds(8 * h, 8), :] = value

        level_two(
            f, lambda rows, u: gathered(tab2, ltab2, side, u, slot + 1, part, rows),
            lambda u, h: None, store, slot + 1, before, after,
        )

    loop(0, sz.slots, body)
    run_copies([(share, share_out), (tab2, tab2_out), (ltab2, ltab2_out)], out_sems)


def one_range(sz, begin, count):
    end = begin + count
    return (0 if begin == 0 else begin - 1), (end if end == sz.slots else end - 1)


def two_range(sz, begin, count):
    end = begin + count
    return (0 if begin == 0 else begin - 2), (end if end == sz.slots else end - 2)


def other_tables_body(sz, spans, extent_ref, halo_same, halo_cross, tab2, ltab2, tab, ltab, *rest):
    wides, pars = rest[:-1], rest[-1]
    core, side, extent, _ = place(extent_ref)
    first = core * sz.slots
    pars[core] = halo_same[halo_same.shape[0] - 1]
    pars[1 - core] = halo_cross[halo_cross.shape[0] - 1]
    build_tables(sz, pars, tab, ltab, 2, extent, first)
    rows = lambda h: pl.ds(8 * h, 8)
    for n, span in enumerate(spans):
        wide1, wide2 = wides[2 * n : 2 * n + 2]
        one, two = one_range(sz, *span), two_range(sz, *span)

        def spread_one(j, x, part):
            for s in range(2):
                for u in range(2):
                    for h in range(2):
                        values = gathered(tab, ltab, s, u, x, part, rows(h))
                        for k, value in enumerate(values):
                            wide1[j, s, u, k, rows(h), :] = value

        def body_one(slot):
            _, _, part = neighbours(sz, slot, first, extent)
            spread_one(slot - one[0], slot + 1, part)

        def body_two(slot):
            _, _, part = neighbours(sz, slot, first, extent)
            for u in range(4):
                for h in range(2):
                    values = gathered(tab2, ltab2, 1 - side, u, slot + 1, part, rows(h))
                    for k, value in enumerate(values):
                        wide2[slot - two[0], u, k, rows(h), :] = value

        loop(*one, body_one)
        _, _, part = neighbours(sz, sz.slots - 1, first, extent)
        count = one[1] - one[0]
        spread_one(count, sz.middle, 0)
        if one[1] == sz.slots:
            spread_one(count + 1, sz.right, part)
        loop(*two, body_two)


def gate_body(*refs):
    pass


def main_body(sz, begin, count, wide, extent_ref, *rest):
    head, last = begin == 0, begin + count == sz.slots
    ins = list(rest)

    def take(n):
        part = ins[:n]
        del ins[:n]
        return part

    same, cross, halo_same, halo_cross, share = take(5)
    tables = take(2 if wide else 4)
    if not head:
        dtail_in, ftail_in, _ = take(3)
    (out,) = take(1)
    if not last:
        dtail_out, ftail_out = take(2)
    d, f, o, out_sem = ins
    core, side, extent, _ = place(extent_ref)
    first = core * sz.slots
    end = begin + count
    low = 0 if head else begin - 2
    zeros = jnp.zeros((ROW, BLK), F32)
    for mine, chunk, halo in ((core, same, halo_same), (1 - core, cross, halo_cross)):
        for i in range(count):
            d[mine, begin + 1 + i] = chunk[i]
        edge = halo[halo.shape[0] - 1]
        if head:
            d[mine, 0] = edge
        if last:
            d[mine, sz.right] = edge
        d[mine, sz.middle] = pltpu.roll(edge, BLK - REACH, 1)
    for s in range(2):
        d[s, sz.zero] = zeros
        f[sz.zero, s] = zeros
        if not head:
            for i in range(2):
                d[s, begin - 1 + i] = dtail_in[s, i]
                f[begin - 2 + i, s] = ftail_in[i, s]

    slots = one_range(sz, begin, count)
    if wide:
        wide1, wide2 = tables

        def coef_at(x, part):
            if isinstance(x, int):
                j = slots[1] - slots[0] + (1 if x == sz.right else 0)
            else:
                j = x - 1 - slots[0]
            return lambda rows, s, u: [wide1[j, s, u, k, rows, :] for k in range(9)]
    else:
        tab1, ltab1, tab2, ltab2 = tables
        coef_at = table_coef(tab1, ltab1)
    level_one_all(sz, d, f, coef_at, slots, head, last, low, end, first, extent)

    def body(slot):
        before, after, part = neighbours(sz, slot, first, extent)
        at = slot - low

        def store(u, h, ri, value):
            o[at, ri, pl.ds(32 * h + u, 8, stride=4), :] = value

        if wide:
            coef = lambda rows, u: [wide2[at, u, k, rows, :] for k in range(9)]
        else:
            coef = lambda rows, u: gathered(tab2, ltab2, 1 - side, u, slot + 1, part, rows)
        level_two(
            f, coef, lambda u, h: [share[slot, ri, u, pl.ds(8 * h, 8), :] for ri in range(2)],
            store, slot + 1, before, after,
        )
        lanes = pl.ds(pl.multiple_of(slot * BLK, BLK), BLK)
        pltpu.make_async_copy(o.at[at], out.at[:, :, lanes], out_sem).start()

    loop(*two_range(sz, begin, count), body)
    if not last:
        for s in range(2):
            for i in range(2):
                dtail_out[s, i] = d[s, end - 1 + i]
                ftail_out[i, s] = f[end - 2 + i, s]
    wait_whole(o, out_sem)


def per_device(images, band_shift, tap_weights, phases, extent_map):
    total_rows = images.shape[2]
    beams = images.shape[1]
    slots = total_rows // BLK // 2
    sz = Sizes(slots, total_rows)
    chunks = CHUNKS
    assert beams == 4 * QRT and sum(chunks) == slots and len(chunks) > 2
    assert sz.used + 6 <= BASE[1] - BASE[0] and BASE[1] + sz.used + 6 <= BLK - 2
    size = lax.axis_size("sub")
    top = 1 << (size.bit_length() - 2)
    swap = lambda x, by: lax.ppermute(x, "sub", [(i, i ^ by) for i in range(size)])
    flat = lambda x: x.reshape(x.shape[0], ROW, BLK)
    extents = (extent_map, SMEM)
    vm = lambda *dims: VMEM(dims, F32)

    half = BLK // 2
    blocks = lambda n: (shape(n, 2, QRT, BLK), ANY)
    lanes = (3 * slots // 2 + 1) * BLK
    count = chunks[0] + 1
    parameters = [
        (band_shift[0], HBM),
        (tap_weights[0].transpose(0, 1, 3, 2), HBM),
        (phases[0].transpose(0, 1, 3, 2), HBM),
    ]
    room = [vm(BLK, BLK), vm(2, half, BLK), vm(2, 2, half, BLK), VMEM((2, 2, half, half), jnp.int32),
            vm(2, 2, 4, half), vm(2, 2, 2, half)]
    first = call(
        functools.partial(head_body, sz), [extents, (images, HBM)] + parameters, [blocks(count)] * 2,
        [vm(2, count, 2, QRT, BLK), vm(2, 3, 2, QRT, BLK)] + room + [DMA((2,)), DMA((3,))],
        grant=56,
    )
    length = -(-(sz.used + 3) // MATES)
    counts = [n for n in chunks[1:] for _ in range(2)] + [length] * MATES + [sz.used]
    *packed, kept, own_par = call(
        functools.partial(near_body, sz, chunks),
        [extents, (images, HBM)] + parameters + [(first[0], ANY)],
        [blocks(n) for n in counts] + [(shape(3, ROW, BLK), VMEM)],
        [vm(n, 2, QRT, BLK) for n in counts] + [vm(2, 2, QRT, lanes)] * 2 + room
        + [DMA((2,)), DMA((2,)), DMA((3,)), DMA((len(counts),))],
        grant=56,
    )
    packed, mates = list(first) + packed[:-MATES], packed[-MATES:]
    mates, kept = [flat(swap(x, 1)) for x in mates], flat(kept)
    send = lambda a, b: (flat(swap(a, top)), flat(swap(b, top ^ 1)))
    def gate(waiting, needed):
        passed = [(x, ANY) for x in waiting]
        out = call(gate_body, passed + [(x, ANY) for x in needed], passed, [], {0: 0, 1: 1})
        return send(*out)

    got = [send(*packed[0:2])]
    got.append(gate(packed[2:4], mates) if GATED else send(*packed[2:4]))
    halo = [(x, VMEM) for x in got[0]]

    tabs1, ltabs1 = (2, 2, 3, QRT, BLK), (2, 2, 2, 6, QRT, BLK)
    tabs2, ltabs2 = (2, 4, 3, QRT, BLK), (2, 2, 4, 6, QRT, BLK)
    shares = (slots, 2, 4, QRT, BLK)
    d_s, f_s = (2, sz.zero + 1, ROW, BLK), (sz.zero + 1, 2, ROW, BLK)
    share, tab2, ltab2 = call(
        functools.partial(local_body, sz, MATES),
        [extents, (kept, HBM), (own_par, HBM)] + [(x, HBM) for x in mates],
        [(shape(*shares), ANY), (shape(*tabs2), ANY), (shape(*ltabs2), ANY)],
        [vm(*d_s), vm(*f_s), vm(2, ROW, BLK), vm(2, 2 * ROW, BLK), vm(*tabs1), vm(*ltabs1),
         vm(*tabs2), vm(*ltabs2), vm(*shares), DMA((7 + MATES,)), DMA((3,))],
        us=LOCAL,
    )

    begins = [sum(chunks[:k]) for k in range(len(chunks))]
    spans = [(begins[k], chunks[k]) for k in range(WIDE, len(chunks))]
    outs = [tabs1, ltabs1]
    for span in spans:
        one, two = one_range(sz, *span), two_range(sz, *span)
        extra = 2 if one[1] == slots else 1
        outs += [(one[1] - one[0] + extra, 2, 2, 9, QRT, BLK), (two[1] - two[0], 4, 9, QRT, BLK)]
    got.append(gate(packed[4:6], [*got[0], share]))
    tab1, ltab1, *wides = call(
        functools.partial(other_tables_body, sz, spans),
        [extents, *halo, (tab2, VMEM), (ltab2, VMEM)],
        [(shape(*s), VMEM) for s in outs], [vm(2, ROW, BLK)], us=HINT,
    )
    tail = [(shape(2, 2, ROW, BLK), VMEM)] * 2
    out = None
    for k, count in enumerate(chunks):
        begin = begins[k]
        head, last = k == 0, k == len(chunks) - 1
        if k >= 1 and k + 2 < len(chunks):
            got.append(gate(packed[2 * k + 4 : 2 * k + 6], [*got[k], dtail]))
        ins = [extents, *((x, VMEM) for x in got[k]), *halo, (share, VMEM)]
        if k >= WIDE:
            ins += [(x, VMEM) for x in wides[2 * (k - WIDE) : 2 * (k - WIDE) + 2]]
        else:
            ins += [(x, VMEM) for x in (tab1, ltab1, tab2, ltab2)]
        outs = [(shape(2, beams, slots * BLK), HBM)]
        aliases = {}
        if not head:
            aliases[len(ins) + 2] = 0
            ins += [(dtail, VMEM), (ftail, VMEM), (out, HBM)]
        if not last:
            outs += tail
        low, top_slot = two_range(sz, begin, count)
        res = call(
            functools.partial(main_body, sz, begin, count, k >= WIDE), ins, outs,
            [vm(*d_s), vm(*f_s), vm(top_slot - low, 2, beams, BLK), DMA], aliases, us=HINT if head else 0.1,
        )
        out = res[0]
        if not last:
            dtail, ftail = res[1:]
    return out


def solution(mesh):
    placed = (
        P(None, None, ("strip", "sub")),
        P(("strip", "sub"), None, None, None, None),
        P(("strip", "sub"), None, None, None, None),
        P(("strip", "sub"), None, None, None, None),
        P("strip"),
    )
    return jax.shard_map(
        per_device,
        mesh=mesh,
        in_specs=placed,
        out_specs=P(None, None, ("strip", "sub")),
        check_vma=False,
    )
```

```python
import functools

import jax
import jax.numpy as jnp
from jax import lax
from jax.experimental import pallas as pl
from jax.experimental.pallas import tpu as pltpu
from jax.sharding import PartitionSpec as P

BLK = 128
QRT = 16
ROW = 2 * QRT
CHUNKS = (18, 9, 5)
HINT = 0
LOCAL = 0
MATES = 3
GATED = True
WIDE = 2

REACH = 10
BASE = (24, 72)


class Sizes:
    def __init__(self, slots, total_rows):
        self.slots = slots
        self.total = total_rows
        self.right = slots + 1
        self.middle = slots + 2
        self.zero = slots + 3
        self.used = slots + 3


F32 = jnp.float32
ANY, HBM, VMEM, SMEM = pl.ANY, pltpu.HBM, pltpu.VMEM, pltpu.SMEM
DMA = pltpu.SemaphoreType.DMA


def shape(*dims):
    return jax.ShapeDtypeStruct(dims, F32)


def call(body, ins, outs, scratch, aliases=None, grant=32, us=0):
    return pl.pallas_call(
        body,
        out_shape=tuple(x for x, _ in outs),
        in_specs=[pl.BlockSpec(memory_space=m) for _, m in ins],
        out_specs=tuple(pl.BlockSpec(memory_space=m) for _, m in outs),
        scratch_shapes=scratch,
        input_output_aliases=aliases or {},
        compiler_params=pltpu.CompilerParams(vmem_limit_bytes=grant * 2**20),
        cost_estimate=pl.CostEstimate(flops=int(us * 10**9) + 1, bytes_accessed=int(us * 3 * 10**6) + 1, transcendentals=0),
    )(*(x for x, _ in ins))


def place(extent_ref):
    pos = lax.axis_index("sub")
    top = lax.axis_size("sub").bit_length() - 2
    core = pos & 1
    side = (pos >> top) & 1
    even = pos - core
    return core, side, extent_ref[even], extent_ref[even ^ (1 << top)]


def wait_whole(ref, sem):
    pltpu.make_async_copy(ref, ref, sem).wait()


def run_copies(copies, sems):
    handles = [pltpu.make_async_copy(src, dst, sems.at[i]) for i, (src, dst) in enumerate(copies)]
    for handle in handles:
        handle.start()
    for handle in handles:
        handle.wait()


def load_rows(images_ref, field_ref, side, sems):
    loads = []
    for part in range(2):
        rows = pl.ds(pl.multiple_of(part * ROW + side * QRT, QRT), QRT)
        source = images_ref.at[:, rows, pl.ds(0, field_ref.shape[-1])]
        loads.append(pltpu.make_async_copy(source, field_ref.at[part], sems.at[part]))
        loads[-1].start()
    return loads


def read_block(field_ref, part, block):
    return field_ref[part, :, :, pl.ds(pl.multiple_of(block * BLK, BLK), BLK)]


def slot_block(extent, slot):
    part = (slot >= extent).astype(jnp.int32)
    return part, slot - part * extent


def halo_blocks(sz, extent, first):
    part, block = slot_block(extent, first)
    left = (part, jnp.maximum(block - 1, 0))
    part, block = slot_block(extent, first + sz.slots - 1)
    return left, (part, block + 1), (0, extent)


def load_parameters(shift_ref, taps_ref, phase_ref, raw_ref, pieces_ref, angles_ref, sems):
    pairs = [(shift_ref, raw_ref), (taps_ref, pieces_ref), (phase_ref, angles_ref)]
    loads = [pltpu.make_async_copy(*pair, sems.at[i]) for i, pair in enumerate(pairs)]
    for load in loads:
        load.start()
    return loads


def turn_parameters(sz, levels, raw_ref, pieces_ref, angles_ref, moved_ref, turned_ref, shifts_ref):
    half = BLK // 2
    for l in levels:
        moved_ref[...] = jnp.zeros((BLK, BLK), F32)
        for s in range(2):
            at = BASE[s] + sz.used
            moved_ref[at : at + 4, 0:half] = pieces_ref[l, s]
            moved_ref[at + 4 : at + 6, 0:half] = angles_ref[l, s]
            shifts_ref[l, s] = jnp.zeros((half, BLK), F32)
            shifts_ref[l, s, :, 0:half] = raw_ref[l, s].astype(F32)
        turned_ref[l] = moved_ref[...].T[0:half]


def window_parameters(sz, turned_ref, shifts_ref, l, row, first, extent, core):
    lane = lax.broadcasted_iota(jnp.int32, (ROW, BLK), 1)
    rows = pl.ds(pl.multiple_of(row, ROW), ROW)
    result = turned_ref[l, rows, :]
    for s in range(2):
        shifts = shifts_ref[l, s, rows, :]
        at = BASE[s]
        turn = lambda by: pltpu.roll(shifts, jnp.bitwise_and(by, BLK - 1), 1)
        inside = jnp.logical_and(lane >= at, lane < at + sz.middle)
        result = jnp.where(inside, turn(at + 1 - first + core * extent), result)
        result = jnp.where(lane == at + sz.middle, turn(at + sz.middle - extent), result)
    return result


def head_body(sz, extent_ref, images_ref, shift_ref, taps_ref, phase_ref, same_ref, cross_ref,
              piece_ref, edge_ref, moved_ref, turned_ref, shifts_ref, raw_ref, pieces_ref, angles_ref,
              sems, par_sems, out_sems):
    core, side, _, other = place(extent_ref)
    windows = (core * sz.slots, (1 - core) * sz.slots)
    small = load_parameters(shift_ref, taps_ref, phase_ref, raw_ref, pieces_ref, angles_ref, par_sems)
    count = piece_ref.shape[1] - 1

    def fetch(part, block, dst, sem):
        rows = pl.ds(pl.multiple_of(part * ROW + (1 - side) * QRT, QRT), QRT)
        lanes = pl.ds(pl.multiple_of(block * BLK, BLK), BLK)
        pltpu.make_async_copy(images_ref.at[:, rows, lanes], dst, sem).start()

    for i in range(2):
        for n, (part, block) in enumerate(halo_blocks(sz, other, windows[i])):
            fetch(part, block, edge_ref.at[i, n], sems.at[0])
    for i in range(2):
        for j in range(count):
            fetch(*slot_block(other, windows[i] + j), piece_ref.at[i, j], sems.at[1])
    homes = (same_ref, cross_ref)
    stores = []

    def put(i, blocks):
        source, target = piece_ref.at[i, blocks], homes[i].at[blocks]
        stores.append(pltpu.make_async_copy(source, target, out_sems.at[len(stores)]))
        stores[-1].start()

    wait_whole(piece_ref.at[:, pl.ds(0, count)], sems.at[1])
    for i in range(2):
        put(i, pl.ds(0, count))
    for load in small:
        load.wait()
    turn_parameters(sz, (0,), raw_ref, pieces_ref, angles_ref, moved_ref, turned_ref, shifts_ref)
    lane = lax.broadcasted_iota(jnp.int32, (ROW, BLK), 1)
    wait_whole(edge_ref, sems.at[0])
    for i in range(2):
        left, right, middle = (edge_ref[i, n].reshape(ROW, BLK) for n in range(3))
        row = (1 - side) * ROW
        result = window_parameters(sz, turned_ref, shifts_ref, 0, row, windows[i], other, core)
        result = jnp.where(lane < 2 * REACH, pltpu.roll(middle, REACH, 1), result)
        result = jnp.where(lane < REACH, right, result)
        result = jnp.where(lane >= BLK - 2, left, result)
        piece_ref[i, count] = result.reshape(2, QRT, BLK)
        put(i, pl.ds(count, 1))
    for store in stores:
        store.wait()


def near_body(sz, chunks, extent_ref, images_ref, shift_ref, taps_ref, phase_ref, _, *rest):
    (*rest, far_ref, field_ref, moved_ref, turned_ref, shifts_ref, raw_ref, pieces_ref, angles_ref,
     far_sems, sems, par_sems, out_sems) = rest
    sends = 2 * len(chunks) - 2
    total = (len(rest) - 1) // 2
    homes, own_par, outs = rest[:total], rest[total], rest[total + 1 :]
    mates, kept = outs[sends:-1], outs[-1]
    core, side, own, other = place(extent_ref)
    windows = (core * sz.slots, (1 - core) * sz.slots)
    far_loads = load_rows(images_ref, far_ref, 1 - side, far_sems)
    loads = load_rows(images_ref, field_ref, side, sems)
    length = mates[0].shape[0]
    small = load_parameters(shift_ref, taps_ref, phase_ref, raw_ref, pieces_ref, angles_ref, par_sems)
    stores = [pltpu.make_async_copy(outs[i], homes[i], out_sems.at[i]) for i in range(len(outs))]
    for load in far_loads:
        load.wait()
    begin = chunks[0]
    for k, count in enumerate(chunks[1:]):
        for i in range(2):
            for j in range(count):
                where = slot_block(other, windows[i] + begin + j)
                outs[2 * k + i][j] = read_block(far_ref, *where)
            stores[2 * k + i].start()
        begin += count
    for load in small:
        load.wait()
    turn_parameters(sz, (0, 1), raw_ref, pieces_ref, angles_ref, moved_ref, turned_ref, shifts_ref)
    for i, level, row in ((0, 0, side * ROW), (1, 1, 0), (2, 1, ROW)):
        made = [
            window_parameters(sz, turned_ref, shifts_ref, level, row, first, own, core)
            for first in windows
        ]
        own_par[i] = made[0]
        mates[-1][length - 3 + i] = made[1].reshape(2, QRT, BLK)
    for load in loads:
        load.wait()

    def put(first, where):
        for x, at in zip((0, sz.right, sz.middle), halo_blocks(sz, own, first)):
            where(x, read_block(field_ref, *at))
        for j in range(sz.slots):
            where(1 + j, read_block(field_ref, *slot_block(own, first + j)))

    def mate_at(x, value):
        mates[x // length][x % length] = value

    def kept_at(x, value):
        kept[x] = value

    put(windows[1], mate_at)
    for store in stores[sends:-1]:
        store.start()
    put(windows[0], kept_at)
    stores[-1].start()
    for store in stores:
        store.wait()


def build_tables(sz, par_ref, tab_ref, ltab_ref, groups, extent, first):
    lane = lax.broadcasted_iota(jnp.int32, (QRT, BLK), 1)
    middle = lane == sz.middle
    even = jnp.logical_or(first + lane - 1 < extent, middle)
    block = jnp.where(even, first - 1 + lane, first - 1 + lane - extent)
    block = jnp.where(middle, extent, block).astype(F32)
    for group in range(groups):
        rows = [par_ref[p, pl.ds(group, QRT, stride=groups), :] for p in range(2)]
        for s in range(2):

            def spread(p, n):
                c = BASE[s] + sz.used + n
                return jnp.broadcast_to(rows[p][:, c : c + 1], (QRT, BLK))

            column = lambda n: jnp.where(even, spread(0, n), spread(1, n))
            tab_ref[s, group, 0] = jnp.where(
                even,
                pltpu.roll(rows[0], BLK - BASE[s], 1),
                pltpu.roll(rows[1], BLK - BASE[s], 1),
            )
            angle = column(4) + column(5) * (block * (BLK / sz.total))
            tab_ref[s, group, 1] = jnp.cos(angle)
            tab_ref[s, group, 2] = jnp.sin(angle)
            for p in range(2):
                angle = spread(p, 5) * (lane.astype(F32) / sz.total)
                ltab_ref[p, s, group, 0] = jnp.cos(angle)
                ltab_ref[p, s, group, 1] = jnp.sin(angle)
                for k in range(4):
                    ltab_ref[p, s, group, 2 + k] = spread(p, k)


def gathered(tab_ref, ltab_ref, s, group, x, part, rows):
    pick = jnp.full((8, BLK), x, jnp.int32)
    shift, cb, sb = (
        jnp.take_along_axis(tab_ref[s, group, k, rows, :], pick, axis=1) for k in range(3)
    )
    cl, sl, *taps = (ltab_ref[part, s, group, k, rows, :] for k in range(6))
    two = shift > 1.5
    one = jnp.where(two, shift - 2.0, shift) > 0.5
    zero = jnp.zeros((8, BLK), F32)
    taps = [zero] + taps + [zero]
    taps = [zero] * 2 + [jnp.where(one, taps[k], taps[k + 1]) for k in range(5)] + [zero] * 2
    weights = [jnp.where(two, taps[k], taps[k + 2]) for k in range(7)]
    return weights + [cb * cl - sb * sl, sb * cl + cb * sl]


def merge_block(sources, load, coef, sums, x, before, after, store):
    lane = lax.broadcasted_iota(jnp.int32, (8, BLK), 1)
    for s in sources:
        moved = []
        for ri in range(2):
            cur, prv, nxt = load(s, x, ri), load(s, before, ri), load(s, after, ri)
            views = [pltpu.roll(jnp.where(lane == BLK - 1, prv, cur), 1, 1), cur]
            for o in range(1, 6):
                views.append(pltpu.roll(jnp.where(lane < o, nxt, cur), BLK - o, 1))
            moved.append(views)
        for u in range(2):
            *weights, cosine, sine = coef(s, u)
            value = []
            for ri in range(2):
                total = weights[0] * moved[ri][0]
                for k in range(1, 7):
                    total = total + weights[k] * moved[ri][k]
                value.append(total)
            real = cosine * value[0] - sine * value[1]
            imag = sine * value[0] + cosine * value[1]
            sums[u] = [real, imag] if sums[u] is None else [sums[u][0] + real, sums[u][1] + imag]
    for u in range(2):
        for ri in range(2):
            store(u, ri, sums[u][ri])


def level_one(d_ref, f_ref, coef, x, before, after):
    for h in range(2):
        rows = lambda ri: pl.ds(QRT * ri + 8 * h, 8)

        def store(u, ri, value):
            f_ref[x, u, rows(ri), :] = value

        merge_block(
            (0, 1), lambda s, at, ri: d_ref[s, at, rows(ri), :],
            lambda s, u: coef(pl.ds(8 * h, 8), s, u), [None, None], x, before, after, store,
        )


def level_two(f_ref, coef, start, store, x, before, after):
    for u1 in range(2):
        for h in range(2):
            sums = [start(2 * u1 + u, h) for u in range(2)]
            merge_block(
                (0,), lambda s, at, ri: f_ref[at, u1, pl.ds(QRT * ri + 8 * h, 8), :],
                lambda s, u: coef(pl.ds(8 * h, 8), 2 * u1 + u), sums, x, before, after,
                lambda u, ri, value: store(2 * u1 + u, h, ri, value),
            )


def neighbours(sz, slot, first, extent):
    where = first + slot
    before = jnp.where(jnp.logical_or(where == 0, where == extent), sz.zero, slot)
    after = jnp.where(where == extent - 1, sz.middle, slot + 2)
    return before, after, (where >= extent).astype(jnp.int32)


def loop(begin, end, body):
    def step(slot, carry):
        body(slot)
        return carry

    lax.fori_loop(begin, end, step, 0, unroll=4)


def level_one_all(sz, d_ref, f_ref, coef_at, slots, left, right, low, high, first, extent):
    part_of = lambda slot: (first + slot >= extent).astype(jnp.int32)

    def body(slot):
        before, after, part = neighbours(sz, slot, first, extent)
        level_one(d_ref, f_ref, coef_at(slot + 1, part), slot + 1, before, after)

    if left:
        level_one(d_ref, f_ref, coef_at(0, part_of(0)), 0, 0, 1)
    loop(*slots, body)
    if right:
        part = part_of(sz.slots - 1)
        level_one(d_ref, f_ref, coef_at(sz.right, part), sz.right, sz.slots, sz.zero)
    before = extent - first

    @pl.when(jnp.logical_and(before > low, before <= high))
    def _():
        level_one(d_ref, f_ref, coef_at(sz.middle, 0), sz.middle, before, sz.zero)


def table_coef(tab, ltab):
    return lambda x, part: (lambda rows, s, u: gathered(tab, ltab, s, u, x, part, rows))


def local_body(sz, pieces, extent_ref, kept, par, *rest):
    mates = rest[:pieces]
    (share_out, tab2_out, ltab2_out, d, f, par1s, par2s, tab, ltab, tab2, ltab2, share,
     sems, out_sems) = rest[pieces:]
    core, side, extent, _ = place(extent_ref)
    first = core * sz.slots
    used = sz.used
    copies = [
        (kept, d.at[core, pl.ds(0, used)]),
        (par.at[0], par1s.at[core]),
        (par.at[1], par2s.at[core, pl.ds(0, ROW)]),
        (par.at[2], par2s.at[core, pl.ds(ROW, ROW)]),
    ]
    length = mates[0].shape[0]
    for i, mate in enumerate(mates):
        count = min(length, used - i * length)
        copies.append((mate.at[pl.ds(0, count)], d.at[1 - core, pl.ds(i * length, count)]))
    copies += [
        (mates[-1].at[length - 3], par1s.at[1 - core]),
        (mates[-1].at[length - 2], par2s.at[1 - core, pl.ds(0, ROW)]),
        (mates[-1].at[length - 1], par2s.at[1 - core, pl.ds(ROW, ROW)]),
    ]
    run_copies(copies, sems)
    zeros = jnp.zeros((ROW, BLK), F32)
    for s in range(2):
        d[s, sz.zero] = zeros
        f[sz.zero, s] = zeros
    build_tables(sz, par1s, tab, ltab, 2, extent, first)
    build_tables(sz, par2s, tab2, ltab2, 4, extent, first)
    level_one_all(
        sz, d, f, table_coef(tab, ltab), (0, sz.slots), True, True, 0, sz.slots, first, extent
    )
    def body(slot):
        before, after, part = neighbours(sz, slot, first, extent)

        def store(u, h, ri, value):
            share[slot, ri, u, pl.ds(8 * h, 8), :] = value

        level_two(
            f, lambda rows, u: gathered(tab2, ltab2, side, u, slot + 1, part, rows),
            lambda u, h: None, store, slot + 1, before, after,
        )

    loop(0, sz.slots, body)
    run_copies([(share, share_out), (tab2, tab2_out), (ltab2, ltab2_out)], out_sems)


def one_range(sz, begin, count):
    end = begin + count
    return (0 if begin == 0 else begin - 1), (end if end == sz.slots else end - 1)


def two_range(sz, begin, count):
    end = begin + count
    return (0 if begin == 0 else begin - 2), (end if end == sz.slots else end - 2)


def other_tables_body(sz, spans, extent_ref, halo_same, halo_cross, tab2, ltab2, tab, ltab, *rest):
    wides, pars = rest[:-1], rest[-1]
    core, side, extent, _ = place(extent_ref)
    first = core * sz.slots
    pars[core] = halo_same[halo_same.shape[0] - 1]
    pars[1 - core] = halo_cross[halo_cross.shape[0] - 1]
    build_tables(sz, pars, tab, ltab, 2, extent, first)
    rows = lambda h: pl.ds(8 * h, 8)
    for n, span in enumerate(spans):
        wide1, wide2 = wides[2 * n : 2 * n + 2]
        one, two = one_range(sz, *span), two_range(sz, *span)

        def spread_one(j, x, part):
            for s in range(2):
                for u in range(2):
                    for h in range(2):
                        values = gathered(tab, ltab, s, u, x, part, rows(h))
                        for k, value in enumerate(values):
                            wide1[j, s, u, k, rows(h), :] = value

        def body_one(slot):
            _, _, part = neighbours(sz, slot, first, extent)
            spread_one(slot - one[0], slot + 1, part)

        def body_two(slot):
            _, _, part = neighbours(sz, slot, first, extent)
            for u in range(4):
                for h in range(2):
                    values = gathered(tab2, ltab2, 1 - side, u, slot + 1, part, rows(h))
                    for k, value in enumerate(values):
                        wide2[slot - two[0], u, k, rows(h), :] = value

        loop(*one, body_one)
        _, _, part = neighbours(sz, sz.slots - 1, first, extent)
        count = one[1] - one[0]
        spread_one(count, sz.middle, 0)
        if one[1] == sz.slots:
            spread_one(count + 1, sz.right, part)
        loop(*two, body_two)


def gate_body(*refs):
    pass


def main_body(sz, begin, count, wide, extent_ref, *rest):
    head, last = begin == 0, begin + count == sz.slots
    ins = list(rest)

    def take(n):
        part = ins[:n]
        del ins[:n]
        return part

    same, cross, halo_same, halo_cross, share = take(5)
    tables = take(2 if wide else 4)
    if not head:
        dtail_in, ftail_in, _ = take(3)
    (out,) = take(1)
    if not last:
        dtail_out, ftail_out = take(2)
    d, f, o, out_sem = ins
    core, side, extent, _ = place(extent_ref)
    first = core * sz.slots
    end = begin + count
    low = 0 if head else begin - 2
    zeros = jnp.zeros((ROW, BLK), F32)
    for mine, chunk, halo in ((core, same, halo_same), (1 - core, cross, halo_cross)):
        for i in range(count):
            d[mine, begin + 1 + i] = chunk[i]
        edge = halo[halo.shape[0] - 1]
        if head:
            d[mine, 0] = edge
        if last:
            d[mine, sz.right] = edge
        d[mine, sz.middle] = pltpu.roll(edge, BLK - REACH, 1)
    for s in range(2):
        d[s, sz.zero] = zeros
        f[sz.zero, s] = zeros
        if not head:
            for i in range(2):
                d[s, begin - 1 + i] = dtail_in[s, i]
                f[begin - 2 + i, s] = ftail_in[i, s]

    slots = one_range(sz, begin, count)
    if wide:
        wide1, wide2 = tables

        def coef_at(x, part):
            if isinstance(x, int):
                j = slots[1] - slots[0] + (1 if x == sz.right else 0)
            else:
                j = x - 1 - slots[0]
            return lambda rows, s, u: [wide1[j, s, u, k, rows, :] for k in range(9)]
    else:
        tab1, ltab1, tab2, ltab2 = tables
        coef_at = table_coef(tab1, ltab1)
    level_one_all(sz, d, f, coef_at, slots, head, last, low, end, first, extent)

    def body(slot):
        before, after, part = neighbours(sz, slot, first, extent)
        at = slot - low

        def store(u, h, ri, value):
            o[at, ri, pl.ds(32 * h + u, 8, stride=4), :] = value

        if wide:
            coef = lambda rows, u: [wide2[at, u, k, rows, :] for k in range(9)]
        else:
            coef = lambda rows, u: gathered(tab2, ltab2, 1 - side, u, slot + 1, part, rows)
        level_two(
            f, coef, lambda u, h: [share[slot, ri, u, pl.ds(8 * h, 8), :] for ri in range(2)],
            store, slot + 1, before, after,
        )
        lanes = pl.ds(pl.multiple_of(slot * BLK, BLK), BLK)
        pltpu.make_async_copy(o.at[at], out.at[:, :, lanes], out_sem).start()

    loop(*two_range(sz, begin, count), body)
    if not last:
        for s in range(2):
            for i in range(2):
                dtail_out[s, i] = d[s, end - 1 + i]
                ftail_out[i, s] = f[end - 2 + i, s]
    wait_whole(o, out_sem)


def per_device(images, band_shift, tap_weights, phases, extent_map):
    total_rows = images.shape[2]
    beams = images.shape[1]
    slots = total_rows // BLK // 2
    sz = Sizes(slots, total_rows)
    chunks = CHUNKS
    assert beams == 4 * QRT and sum(chunks) == slots and len(chunks) > 2
    assert sz.used + 6 <= BASE[1] - BASE[0] and BASE[1] + sz.used + 6 <= BLK - 2
    size = lax.axis_size("sub")
    top = 1 << (size.bit_length() - 2)
    swap = lambda x, by: lax.ppermute(x, "sub", [(i, i ^ by) for i in range(size)])
    flat = lambda x: x.reshape(x.shape[0], ROW, BLK)
    extents = (extent_map, SMEM)
    vm = lambda *dims: VMEM(dims, F32)

    half = BLK // 2
    blocks = lambda n: (shape(n, 2, QRT, BLK), ANY)
    lanes = (3 * slots // 2 + 1) * BLK
    count = chunks[0] + 1
    parameters = [
        (band_shift[0], HBM),
        (tap_weights[0].transpose(0, 1, 3, 2), HBM),
        (phases[0].transpose(0, 1, 3, 2), HBM),
    ]
    room = [vm(BLK, BLK), vm(2, half, BLK), vm(2, 2, half, BLK), VMEM((2, 2, half, half), jnp.int32),
            vm(2, 2, 4, half), vm(2, 2, 2, half)]
    first = call(
        functools.partial(head_body, sz), [extents, (images, HBM)] + parameters, [blocks(count)] * 2,
        [vm(2, count, 2, QRT, BLK), vm(2, 3, 2, QRT, BLK)] + room
        + [DMA((2,)), DMA((3,)), DMA((4,))],
        grant=56,
    )
    length = -(-(sz.used + 3) // MATES)
    counts = [n for n in chunks[1:] for _ in range(2)] + [length] * MATES + [sz.used]
    *packed, kept, own_par = call(
        functools.partial(near_body, sz, chunks),
        [extents, (images, HBM)] + parameters + [(first[0], ANY)],
        [blocks(n) for n in counts] + [(shape(3, ROW, BLK), VMEM)],
        [vm(n, 2, QRT, BLK) for n in counts] + [vm(2, 2, QRT, lanes)] * 2 + room
        + [DMA((2,)), DMA((2,)), DMA((3,)), DMA((len(counts),))],
        grant=56,
    )
    packed, mates = list(first) + packed[:-MATES], packed[-MATES:]
    mates, kept = [flat(swap(x, 1)) for x in mates], flat(kept)
    send = lambda a, b: (flat(swap(a, top)), flat(swap(b, top ^ 1)))
    def gate(waiting, needed):
        passed = [(x, ANY) for x in waiting]
        out = call(gate_body, passed + [(x, ANY) for x in needed], passed, [], {0: 0, 1: 1})
        return send(*out)

    got = [send(*packed[0:2])]
    got.append(gate(packed[2:4], mates) if GATED else send(*packed[2:4]))
    halo = [(x, VMEM) for x in got[0]]

    tabs1, ltabs1 = (2, 2, 3, QRT, BLK), (2, 2, 2, 6, QRT, BLK)
    tabs2, ltabs2 = (2, 4, 3, QRT, BLK), (2, 2, 4, 6, QRT, BLK)
    shares = (slots, 2, 4, QRT, BLK)
    d_s, f_s = (2, sz.zero + 1, ROW, BLK), (sz.zero + 1, 2, ROW, BLK)
    share, tab2, ltab2 = call(
        functools.partial(local_body, sz, MATES),
        [extents, (kept, HBM), (own_par, HBM)] + [(x, HBM) for x in mates],
        [(shape(*shares), ANY), (shape(*tabs2), ANY), (shape(*ltabs2), ANY)],
        [vm(*d_s), vm(*f_s), vm(2, ROW, BLK), vm(2, 2 * ROW, BLK), vm(*tabs1), vm(*ltabs1),
         vm(*tabs2), vm(*ltabs2), vm(*shares), DMA((7 + MATES,)), DMA((3,))],
        us=LOCAL,
    )

    begins = [sum(chunks[:k]) for k in range(len(chunks))]
    spans = [(begins[k], chunks[k]) for k in range(WIDE, len(chunks))]
    outs = [tabs1, ltabs1]
    for span in spans:
        one, two = one_range(sz, *span), two_range(sz, *span)
        extra = 2 if one[1] == slots else 1
        outs += [(one[1] - one[0] + extra, 2, 2, 9, QRT, BLK), (two[1] - two[0], 4, 9, QRT, BLK)]
    got.append(gate(packed[4:6], [*got[0], share]))
    tab1, ltab1, *wides = call(
        functools.partial(other_tables_body, sz, spans),
        [extents, *halo, (tab2, VMEM), (ltab2, VMEM)],
        [(shape(*s), VMEM) for s in outs], [vm(2, ROW, BLK)], us=HINT,
    )
    tail = [(shape(2, 2, ROW, BLK), VMEM)] * 2
    out = None
    for k, count in enumerate(chunks):
        begin = begins[k]
        head, last = k == 0, k == len(chunks) - 1
        if k >= 1 and k + 2 < len(chunks):
            got.append(gate(packed[2 * k + 4 : 2 * k + 6], [*got[k], dtail]))
        ins = [extents, *((x, VMEM) for x in got[k]), *halo, (share, VMEM)]
        if k >= WIDE:
            ins += [(x, VMEM) for x in wides[2 * (k - WIDE) : 2 * (k - WIDE) + 2]]
        else:
            ins += [(x, VMEM) for x in (tab1, ltab1, tab2, ltab2)]
        outs = [(shape(2, beams, slots * BLK), HBM)]
        aliases = {}
        if not head:
            aliases[len(ins) + 2] = 0
            ins += [(dtail, VMEM), (ftail, VMEM), (out, HBM)]
        if not last:
            outs += tail
        low, top_slot = two_range(sz, begin, count)
        res = call(
            functools.partial(main_body, sz, begin, count, k >= WIDE), ins, outs,
            [vm(*d_s), vm(*f_s), vm(top_slot - low, 2, beams, BLK), DMA], aliases, us=HINT if head else 0.1,
        )
        out = res[0]
        if not last:
            dtail, ftail = res[1:]
    return out


def solution(mesh):
    placed = (
        P(None, None, ("strip", "sub")),
        P(("strip", "sub"), None, None, None, None),
        P(("strip", "sub"), None, None, None, None),
        P(("strip", "sub"), None, None, None, None),
        P("strip"),
    )
    return jax.shard_map(
        per_device,
        mesh=mesh,
        in_specs=placed,
        out_specs=P(None, None, ("strip", "sub")),
        check_vma=False,
    )
```

```python
import functools

import jax
import jax.numpy as jnp
from jax import lax
from jax.experimental import pallas as pl
from jax.experimental.pallas import tpu as pltpu
from jax.sharding import PartitionSpec as P

BLK = 128
QRT = 16
ROW = 2 * QRT
CHUNKS = (18, 9, 5)
HINT = 0
LOCAL = 0
MATES = 3
GATED = True
WIDE = 2

REACH = 10
BASE = (24, 72)


class Sizes:
    def __init__(self, slots, total_rows):
        self.slots = slots
        self.total = total_rows
        self.right = slots + 1
        self.middle = slots + 2
        self.zero = slots + 3
        self.used = slots + 3


F32 = jnp.float32
ANY, HBM, VMEM, SMEM = pl.ANY, pltpu.HBM, pltpu.VMEM, pltpu.SMEM
DMA = pltpu.SemaphoreType.DMA


def shape(*dims):
    return jax.ShapeDtypeStruct(dims, F32)


def call(body, ins, outs, scratch, aliases=None, grant=32, us=0):
    return pl.pallas_call(
        body,
        out_shape=tuple(x for x, _ in outs),
        in_specs=[pl.BlockSpec(memory_space=m) for _, m in ins],
        out_specs=tuple(pl.BlockSpec(memory_space=m) for _, m in outs),
        scratch_shapes=scratch,
        input_output_aliases=aliases or {},
        compiler_params=pltpu.CompilerParams(vmem_limit_bytes=grant * 2**20),
        cost_estimate=pl.CostEstimate(flops=int(us * 10**9) + 1, bytes_accessed=int(us * 3 * 10**6) + 1, transcendentals=0),
    )(*(x for x, _ in ins))


def place(extent_ref):
    pos = lax.axis_index("sub")
    top = lax.axis_size("sub").bit_length() - 2
    core = pos & 1
    side = (pos >> top) & 1
    even = pos - core
    return core, side, extent_ref[even], extent_ref[even ^ (1 << top)]


def wait_whole(ref, sem):
    pltpu.make_async_copy(ref, ref, sem).wait()


def run_copies(copies, sems):
    handles = [pltpu.make_async_copy(src, dst, sems.at[i]) for i, (src, dst) in enumerate(copies)]
    for handle in handles:
        handle.start()
    for handle in handles:
        handle.wait()


def load_rows(images_ref, field_ref, side, sems):
    loads = []
    for part in range(2):
        rows = pl.ds(pl.multiple_of(part * ROW + side * QRT, QRT), QRT)
        source = images_ref.at[:, rows, pl.ds(0, field_ref.shape[-1])]
        loads.append(pltpu.make_async_copy(source, field_ref.at[part], sems.at[part]))
        loads[-1].start()
    return loads


def read_block(field_ref, part, block):
    return field_ref[part, :, :, pl.ds(pl.multiple_of(block * BLK, BLK), BLK)]


def slot_block(extent, slot):
    part = (slot >= extent).astype(jnp.int32)
    return part, slot - part * extent


def halo_blocks(sz, extent, first):
    part, block = slot_block(extent, first)
    left = (part, jnp.maximum(block - 1, 0))
    part, block = slot_block(extent, first + sz.slots - 1)
    return left, (part, block + 1), (0, extent)


def load_parameters(shift_ref, taps_ref, phase_ref, raw_ref, pieces_ref, angles_ref, sems):
    pairs = [(shift_ref, raw_ref), (taps_ref, pieces_ref), (phase_ref, angles_ref)]
    loads = [pltpu.make_async_copy(*pair, sems.at[i]) for i, pair in enumerate(pairs)]
    for load in loads:
        load.start()
    return loads


def turn_parameters(sz, levels, raw_ref, pieces_ref, angles_ref, moved_ref, turned_ref, shifts_ref):
    half = BLK // 2
    for l in levels:
        moved_ref[...] = jnp.zeros((BLK, BLK), F32)
        for s in range(2):
            at = BASE[s] + sz.used
            moved_ref[at : at + 4, 0:half] = pieces_ref[l, s]
            moved_ref[at + 4 : at + 6, 0:half] = angles_ref[l, s]
            shifts_ref[l, s] = jnp.zeros((half, BLK), F32)
            shifts_ref[l, s, :, 0:half] = raw_ref[l, s].astype(F32)
        turned_ref[l] = moved_ref[...].T[0:half]


def window_parameters(sz, turned_ref, shifts_ref, l, row, first, extent, core):
    lane = lax.broadcasted_iota(jnp.int32, (ROW, BLK), 1)
    rows = pl.ds(pl.multiple_of(row, ROW), ROW)
    result = turned_ref[l, rows, :]
    for s in range(2):
        shifts = shifts_ref[l, s, rows, :]
        at = BASE[s]
        turn = lambda by: pltpu.roll(shifts, jnp.bitwise_and(by, BLK - 1), 1)
        inside = jnp.logical_and(lane >= at, lane < at + sz.middle)
        result = jnp.where(inside, turn(at + 1 - first + core * extent), result)
        result = jnp.where(lane == at + sz.middle, turn(at + sz.middle - extent), result)
    return result


def head_body(sz, extent_ref, images_ref, shift_ref, taps_ref, phase_ref, same_ref, cross_ref,
              piece_ref, edge_ref, moved_ref, turned_ref, shifts_ref, raw_ref, pieces_ref, angles_ref,
              sems, par_sems, out_sems):
    core, side, _, other = place(extent_ref)
    windows = (core * sz.slots, (1 - core) * sz.slots)
    small = load_parameters(shift_ref, taps_ref, phase_ref, raw_ref, pieces_ref, angles_ref, par_sems)
    count = piece_ref.shape[1] - 1

    def fetch(part, block, dst, sem):
        rows = pl.ds(pl.multiple_of(part * ROW + (1 - side) * QRT, QRT), QRT)
        lanes = pl.ds(pl.multiple_of(block * BLK, BLK), BLK)
        pltpu.make_async_copy(images_ref.at[:, rows, lanes], dst, sem).start()

    for i in range(2):
        for n, (part, block) in enumerate(halo_blocks(sz, other, windows[i])):
            fetch(part, block, edge_ref.at[i, n], sems.at[0])
    for i in range(2):
        for j in range(count):
            fetch(*slot_block(other, windows[i] + j), piece_ref.at[i, j], sems.at[1])
    homes = (same_ref, cross_ref)
    stores = []

    def put(i, blocks):
        source, target = piece_ref.at[i, blocks], homes[i].at[blocks]
        stores.append(pltpu.make_async_copy(source, target, out_sems.at[len(stores)]))
        stores[-1].start()

    wait_whole(piece_ref.at[:, pl.ds(0, count)], sems.at[1])
    for i in range(2):
        put(i, pl.ds(0, count))
    for load in small:
        load.wait()
    turn_parameters(sz, (0,), raw_ref, pieces_ref, angles_ref, moved_ref, turned_ref, shifts_ref)
    lane = lax.broadcasted_iota(jnp.int32, (ROW, BLK), 1)
    wait_whole(edge_ref, sems.at[0])
    for i in range(2):
        left, right, middle = (edge_ref[i, n].reshape(ROW, BLK) for n in range(3))
        row = (1 - side) * ROW
        result = window_parameters(sz, turned_ref, shifts_ref, 0, row, windows[i], other, core)
        result = jnp.where(lane < 2 * REACH, pltpu.roll(middle, REACH, 1), result)
        result = jnp.where(lane < REACH, right, result)
        result = jnp.where(lane >= BLK - 2, left, result)
        piece_ref[i, count] = result.reshape(2, QRT, BLK)
        put(i, pl.ds(count, 1))
    for store in stores:
        store.wait()


def near_body(sz, chunks, extent_ref, images_ref, shift_ref, taps_ref, phase_ref, _, *rest):
    (*rest, far_ref, field_ref, moved_ref, turned_ref, shifts_ref, raw_ref, pieces_ref, angles_ref,
     far_sems, sems, par_sems, out_sems) = rest
    sends = 2 * len(chunks) - 2
    total = (len(rest) - 1) // 2
    homes, own_par, outs = rest[:total], rest[total], rest[total + 1 :]
    mates, kept = outs[sends:-1], outs[-1]
    core, side, own, other = place(extent_ref)
    windows = (core * sz.slots, (1 - core) * sz.slots)
    far_loads = load_rows(images_ref, far_ref, 1 - side, far_sems)
    loads = load_rows(images_ref, field_ref, side, sems)
    length = mates[0].shape[0]
    small = load_parameters(shift_ref, taps_ref, phase_ref, raw_ref, pieces_ref, angles_ref, par_sems)
    stores = [pltpu.make_async_copy(outs[i], homes[i], out_sems.at[i]) for i in range(len(outs))]
    for load in far_loads:
        load.wait()
    begin = chunks[0]
    for k, count in enumerate(chunks[1:]):
        for i in range(2):
            for j in range(count):
                where = slot_block(other, windows[i] + begin + j)
                outs[2 * k + i][j] = read_block(far_ref, *where)
            stores[2 * k + i].start()
        begin += count
    for load in small:
        load.wait()
    turn_parameters(sz, (0, 1), raw_ref, pieces_ref, angles_ref, moved_ref, turned_ref, shifts_ref)
    for i, level, row in ((0, 0, side * ROW), (1, 1, 0), (2, 1, ROW)):
        made = [
            window_parameters(sz, turned_ref, shifts_ref, level, row, first, own, core)
            for first in windows
        ]
        own_par[i] = made[0]
        mates[-1][length - 3 + i] = made[1].reshape(2, QRT, BLK)
    for load in loads:
        load.wait()

    def put(first, where):
        for x, at in zip((0, sz.right, sz.middle), halo_blocks(sz, own, first)):
            where(x, read_block(field_ref, *at))
        for j in range(sz.slots):
            where(1 + j, read_block(field_ref, *slot_block(own, first + j)))

    def mate_at(x, value):
        mates[x // length][x % length] = value

    def kept_at(x, value):
        kept[x] = value

    put(windows[1], mate_at)
    for store in stores[sends:-1]:
        store.start()
    put(windows[0], kept_at)
    stores[-1].start()
    for store in stores:
        store.wait()


def build_tables(sz, par_ref, tab_ref, ltab_ref, groups, extent, first):
    lane = lax.broadcasted_iota(jnp.int32, (QRT, BLK), 1)
    middle = lane == sz.middle
    even = jnp.logical_or(first + lane - 1 < extent, middle)
    block = jnp.where(even, first - 1 + lane, first - 1 + lane - extent)
    block = jnp.where(middle, extent, block).astype(F32)
    for group in range(groups):
        rows = [par_ref[p, pl.ds(group, QRT, stride=groups), :] for p in range(2)]
        for s in range(2):

            def spread(p, n):
                c = BASE[s] + sz.used + n
                return jnp.broadcast_to(rows[p][:, c : c + 1], (QRT, BLK))

            column = lambda n: jnp.where(even, spread(0, n), spread(1, n))
            tab_ref[s, group, 0] = jnp.where(
                even,
                pltpu.roll(rows[0], BLK - BASE[s], 1),
                pltpu.roll(rows[1], BLK - BASE[s], 1),
            )
            angle = column(4) + column(5) * (block * (BLK / sz.total))
            tab_ref[s, group, 1] = jnp.cos(angle)
            tab_ref[s, group, 2] = jnp.sin(angle)
            for p in range(2):
                angle = spread(p, 5) * (lane.astype(F32) / sz.total)
                ltab_ref[p, s, group, 0] = jnp.cos(angle)
                ltab_ref[p, s, group, 1] = jnp.sin(angle)
                for k in range(4):
                    ltab_ref[p, s, group, 2 + k] = spread(p, k)


def gathered(tab_ref, ltab_ref, s, group, x, part, rows):
    pick = jnp.full((8, BLK), x, jnp.int32)
    shift, cb, sb = (
        jnp.take_along_axis(tab_ref[s, group, k, rows, :], pick, axis=1) for k in range(3)
    )
    cl, sl, *taps = (ltab_ref[part, s, group, k, rows, :] for k in range(6))
    two = shift > 1.5
    one = jnp.where(two, shift - 2.0, shift) > 0.5
    zero = jnp.zeros((8, BLK), F32)
    taps = [zero] + taps + [zero]
    taps = [zero] * 2 + [jnp.where(one, taps[k], taps[k + 1]) for k in range(5)] + [zero] * 2
    weights = [jnp.where(two, taps[k], taps[k + 2]) for k in range(7)]
    return weights + [cb * cl - sb * sl, sb * cl + cb * sl]


def merge_block(sources, load, coef, sums, x, before, after, store):
    lane = lax.broadcasted_iota(jnp.int32, (8, BLK), 1)
    for s in sources:
        moved = []
        for ri in range(2):
            cur, prv, nxt = load(s, x, ri), load(s, before, ri), load(s, after, ri)
            views = [pltpu.roll(jnp.where(lane == BLK - 1, prv, cur), 1, 1), cur]
            for o in range(1, 6):
                views.append(pltpu.roll(jnp.where(lane < o, nxt, cur), BLK - o, 1))
            moved.append(views)
        for u in range(2):
            *weights, cosine, sine = coef(s, u)
            value = []
            for ri in range(2):
                total = weights[0] * moved[ri][0]
                for k in range(1, 7):
                    total = total + weights[k] * moved[ri][k]
                value.append(total)
            real = cosine * value[0] - sine * value[1]
            imag = sine * value[0] + cosine * value[1]
            sums[u] = [real, imag] if sums[u] is None else [sums[u][0] + real, sums[u][1] + imag]
    for u in range(2):
        for ri in range(2):
            store(u, ri, sums[u][ri])


def level_one(d_ref, f_ref, coef, x, before, after):
    for h in range(2):
        rows = lambda ri: pl.ds(QRT * ri + 8 * h, 8)

        def store(u, ri, value):
            f_ref[x, u, rows(ri), :] = value

        merge_block(
            (0, 1), lambda s, at, ri: d_ref[s, at, rows(ri), :],
            lambda s, u: coef(pl.ds(8 * h, 8), s, u), [None, None], x, before, after, store,
        )


def level_two(f_ref, coef, start, store, x, before, after):
    for u1 in range(2):
        for h in range(2):
            sums = [start(2 * u1 + u, h) for u in range(2)]
            merge_block(
                (0,), lambda s, at, ri: f_ref[at, u1, pl.ds(QRT * ri + 8 * h, 8), :],
                lambda s, u: coef(pl.ds(8 * h, 8), 2 * u1 + u), sums, x, before, after,
                lambda u, ri, value: store(2 * u1 + u, h, ri, value),
            )


def neighbours(sz, slot, first, extent):
    where = first + slot
    before = jnp.where(jnp.logical_or(where == 0, where == extent), sz.zero, slot)
    after = jnp.where(where == extent - 1, sz.middle, slot + 2)
    return before, after, (where >= extent).astype(jnp.int32)


def loop(begin, end, body):
    def step(slot, carry):
        body(slot)
        return carry

    lax.fori_loop(begin, end, step, 0, unroll=3 if (end - begin) % 3 == 0 else 4)


def level_one_all(sz, d_ref, f_ref, coef_at, slots, left, right, low, high, first, extent):
    part_of = lambda slot: (first + slot >= extent).astype(jnp.int32)

    def body(slot):
        before, after, part = neighbours(sz, slot, first, extent)
        level_one(d_ref, f_ref, coef_at(slot + 1, part), slot + 1, before, after)

    if left:
        level_one(d_ref, f_ref, coef_at(0, part_of(0)), 0, 0, 1)
    loop(*slots, body)
    if right:
        part = part_of(sz.slots - 1)
        level_one(d_ref, f_ref, coef_at(sz.right, part), sz.right, sz.slots, sz.zero)
    before = extent - first

    @pl.when(jnp.logical_and(before > low, before <= high))
    def _():
        level_one(d_ref, f_ref, coef_at(sz.middle, 0), sz.middle, before, sz.zero)


def table_coef(tab, ltab):
    return lambda x, part: (lambda rows, s, u: gathered(tab, ltab, s, u, x, part, rows))


def local_body(sz, pieces, extent_ref, kept, par, *rest):
    mates = rest[:pieces]
    (share_out, tab2_out, ltab2_out, d, f, par1s, par2s, tab, ltab, tab2, ltab2, share,
     sems, out_sems) = rest[pieces:]
    core, side, extent, _ = place(extent_ref)
    first = core * sz.slots
    used = sz.used
    copies = [
        (kept, d.at[core, pl.ds(0, used)]),
        (par.at[0], par1s.at[core]),
        (par.at[1], par2s.at[core, pl.ds(0, ROW)]),
        (par.at[2], par2s.at[core, pl.ds(ROW, ROW)]),
    ]
    length = mates[0].shape[0]
    for i, mate in enumerate(mates):
        count = min(length, used - i * length)
        copies.append((mate.at[pl.ds(0, count)], d.at[1 - core, pl.ds(i * length, count)]))
    copies += [
        (mates[-1].at[length - 3], par1s.at[1 - core]),
        (mates[-1].at[length - 2], par2s.at[1 - core, pl.ds(0, ROW)]),
        (mates[-1].at[length - 1], par2s.at[1 - core, pl.ds(ROW, ROW)]),
    ]
    run_copies(copies, sems)
    zeros = jnp.zeros((ROW, BLK), F32)
    for s in range(2):
        d[s, sz.zero] = zeros
        f[sz.zero, s] = zeros
    build_tables(sz, par1s, tab, ltab, 2, extent, first)
    build_tables(sz, par2s, tab2, ltab2, 4, extent, first)
    level_one_all(
        sz, d, f, table_coef(tab, ltab), (0, sz.slots), True, True, 0, sz.slots, first, extent
    )
    def body(slot):
        before, after, part = neighbours(sz, slot, first, extent)

        def store(u, h, ri, value):
            share[slot, ri, u, pl.ds(8 * h, 8), :] = value

        level_two(
            f, lambda rows, u: gathered(tab2, ltab2, side, u, slot + 1, part, rows),
            lambda u, h: None, store, slot + 1, before, after,
        )

    loop(0, sz.slots, body)
    run_copies([(share, share_out), (tab2, tab2_out), (ltab2, ltab2_out)], out_sems)


def one_range(sz, begin, count):
    end = begin + count
    return (0 if begin == 0 else begin - 1), (end if end == sz.slots else end - 1)


def two_range(sz, begin, count):
    end = begin + count
    return (0 if begin == 0 else begin - 2), (end if end == sz.slots else end - 2)


def other_tables_body(sz, spans, extent_ref, halo_same, halo_cross, tab2, ltab2, tab, ltab, *rest):
    wides, pars = rest[:-1], rest[-1]
    core, side, extent, _ = place(extent_ref)
    first = core * sz.slots
    pars[core] = halo_same[halo_same.shape[0] - 1]
    pars[1 - core] = halo_cross[halo_cross.shape[0] - 1]
    build_tables(sz, pars, tab, ltab, 2, extent, first)
    rows = lambda h: pl.ds(8 * h, 8)
    for n, span in enumerate(spans):
        wide1, wide2 = wides[2 * n : 2 * n + 2]
        one, two = one_range(sz, *span), two_range(sz, *span)

        def spread_one(j, x, part):
            for s in range(2):
                for u in range(2):
                    for h in range(2):
                        values = gathered(tab, ltab, s, u, x, part, rows(h))
                        for k, value in enumerate(values):
                            wide1[j, s, u, k, rows(h), :] = value

        def body_one(slot):
            _, _, part = neighbours(sz, slot, first, extent)
            spread_one(slot - one[0], slot + 1, part)

        def body_two(slot):
            _, _, part = neighbours(sz, slot, first, extent)
            for u in range(4):
                for h in range(2):
                    values = gathered(tab2, ltab2, 1 - side, u, slot + 1, part, rows(h))
                    for k, value in enumerate(values):
                        wide2[slot - two[0], u, k, rows(h), :] = value

        loop(*one, body_one)
        _, _, part = neighbours(sz, sz.slots - 1, first, extent)
        count = one[1] - one[0]
        spread_one(count, sz.middle, 0)
        if one[1] == sz.slots:
            spread_one(count + 1, sz.right, part)
        loop(*two, body_two)


def gate_body(*refs):
    pass


def main_body(sz, begin, count, wide, extent_ref, *rest):
    head, last = begin == 0, begin + count == sz.slots
    ins = list(rest)

    def take(n):
        part = ins[:n]
        del ins[:n]
        return part

    same, cross, halo_same, halo_cross, share = take(5)
    tables = take(2 if wide else 4)
    if not head:
        dtail_in, ftail_in, _ = take(3)
    (out,) = take(1)
    if not last:
        dtail_out, ftail_out = take(2)
    d, f, o, out_sem = ins
    core, side, extent, _ = place(extent_ref)
    first = core * sz.slots
    end = begin + count
    low = 0 if head else begin - 2
    zeros = jnp.zeros((ROW, BLK), F32)
    for mine, chunk, halo in ((core, same, halo_same), (1 - core, cross, halo_cross)):
        for i in range(count):
            d[mine, begin + 1 + i] = chunk[i]
        edge = halo[halo.shape[0] - 1]
        if head:
            d[mine, 0] = edge
        if last:
            d[mine, sz.right] = edge
        d[mine, sz.middle] = pltpu.roll(edge, BLK - REACH, 1)
    for s in range(2):
        d[s, sz.zero] = zeros
        f[sz.zero, s] = zeros
        if not head:
            for i in range(2):
                d[s, begin - 1 + i] = dtail_in[s, i]
                f[begin - 2 + i, s] = ftail_in[i, s]

    slots = one_range(sz, begin, count)
    if wide:
        wide1, wide2 = tables

        def coef_at(x, part):
            if isinstance(x, int):
                j = slots[1] - slots[0] + (1 if x == sz.right else 0)
            else:
                j = x - 1 - slots[0]
            return lambda rows, s, u: [wide1[j, s, u, k, rows, :] for k in range(9)]
    else:
        tab1, ltab1, tab2, ltab2 = tables
        coef_at = table_coef(tab1, ltab1)
    level_one_all(sz, d, f, coef_at, slots, head, last, low, end, first, extent)

    def body(slot):
        before, after, part = neighbours(sz, slot, first, extent)
        at = slot - low

        def store(u, h, ri, value):
            o[at, ri, pl.ds(32 * h + u, 8, stride=4), :] = value

        if wide:
            coef = lambda rows, u: [wide2[at, u, k, rows, :] for k in range(9)]
        else:
            coef = lambda rows, u: gathered(tab2, ltab2, 1 - side, u, slot + 1, part, rows)
        level_two(
            f, coef, lambda u, h: [share[slot, ri, u, pl.ds(8 * h, 8), :] for ri in range(2)],
            store, slot + 1, before, after,
        )
        lanes = pl.ds(pl.multiple_of(slot * BLK, BLK), BLK)
        pltpu.make_async_copy(o.at[at], out.at[:, :, lanes], out_sem).start()

    loop(*two_range(sz, begin, count), body)
    if not last:
        for s in range(2):
            for i in range(2):
                dtail_out[s, i] = d[s, end - 1 + i]
                ftail_out[i, s] = f[end - 2 + i, s]
    wait_whole(o, out_sem)


def per_device(images, band_shift, tap_weights, phases, extent_map):
    total_rows = images.shape[2]
    beams = images.shape[1]
    slots = total_rows // BLK // 2
    sz = Sizes(slots, total_rows)
    chunks = CHUNKS
    assert beams == 4 * QRT and sum(chunks) == slots and len(chunks) > 2
    assert sz.used + 6 <= BASE[1] - BASE[0] and BASE[1] + sz.used + 6 <= BLK - 2
    size = lax.axis_size("sub")
    top = 1 << (size.bit_length() - 2)
    swap = lambda x, by: lax.ppermute(x, "sub", [(i, i ^ by) for i in range(size)])
    flat = lambda x: x.reshape(x.shape[0], ROW, BLK)
    extents = (extent_map, SMEM)
    vm = lambda *dims: VMEM(dims, F32)

    half = BLK // 2
    blocks = lambda n: (shape(n, 2, QRT, BLK), ANY)
    lanes = (3 * slots // 2 + 1) * BLK
    count = chunks[0] + 1
    parameters = [
        (band_shift[0], HBM),
        (tap_weights[0].transpose(0, 1, 3, 2), HBM),
        (phases[0].transpose(0, 1, 3, 2), HBM),
    ]
    room = [vm(BLK, BLK), vm(2, half, BLK), vm(2, 2, half, BLK), VMEM((2, 2, half, half), jnp.int32),
            vm(2, 2, 4, half), vm(2, 2, 2, half)]
    first = call(
        functools.partial(head_body, sz), [extents, (images, HBM)] + parameters, [blocks(count)] * 2,
        [vm(2, count, 2, QRT, BLK), vm(2, 3, 2, QRT, BLK)] + room
        + [DMA((2,)), DMA((3,)), DMA((4,))],
        grant=56,
    )
    length = -(-(sz.used + 3) // MATES)
    counts = [n for n in chunks[1:] for _ in range(2)] + [length] * MATES + [sz.used]
    *packed, kept, own_par = call(
        functools.partial(near_body, sz, chunks),
        [extents, (images, HBM)] + parameters + [(first[0], ANY)],
        [blocks(n) for n in counts] + [(shape(3, ROW, BLK), VMEM)],
        [vm(n, 2, QRT, BLK) for n in counts] + [vm(2, 2, QRT, lanes)] * 2 + room
        + [DMA((2,)), DMA((2,)), DMA((3,)), DMA((len(counts),))],
        grant=56,
    )
    packed, mates = list(first) + packed[:-MATES], packed[-MATES:]
    mates, kept = [flat(swap(x, 1)) for x in mates], flat(kept)
    send = lambda a, b: (flat(swap(a, top)), flat(swap(b, top ^ 1)))
    def gate(waiting, needed):
        passed = [(x, ANY) for x in waiting]
        out = call(gate_body, passed + [(x, ANY) for x in needed], passed, [], {0: 0, 1: 1})
        return send(*out)

    got = [send(*packed[0:2])]
    got.append(gate(packed[2:4], mates) if GATED else send(*packed[2:4]))
    halo = [(x, VMEM) for x in got[0]]

    tabs1, ltabs1 = (2, 2, 3, QRT, BLK), (2, 2, 2, 6, QRT, BLK)
    tabs2, ltabs2 = (2, 4, 3, QRT, BLK), (2, 2, 4, 6, QRT, BLK)
    shares = (slots, 2, 4, QRT, BLK)
    d_s, f_s = (2, sz.zero + 1, ROW, BLK), (sz.zero + 1, 2, ROW, BLK)
    share, tab2, ltab2 = call(
        functools.partial(local_body, sz, MATES),
        [extents, (kept, HBM), (own_par, HBM)] + [(x, HBM) for x in mates],
        [(shape(*shares), ANY), (shape(*tabs2), ANY), (shape(*ltabs2), ANY)],
        [vm(*d_s), vm(*f_s), vm(2, ROW, BLK), vm(2, 2 * ROW, BLK), vm(*tabs1), vm(*ltabs1),
         vm(*tabs2), vm(*ltabs2), vm(*shares), DMA((7 + MATES,)), DMA((3,))],
        us=LOCAL,
    )

    begins = [sum(chunks[:k]) for k in range(len(chunks))]
    spans = [(begins[k], chunks[k]) for k in range(WIDE, len(chunks))]
    outs = [tabs1, ltabs1]
    for span in spans:
        one, two = one_range(sz, *span), two_range(sz, *span)
        extra = 2 if one[1] == slots else 1
        outs += [(one[1] - one[0] + extra, 2, 2, 9, QRT, BLK), (two[1] - two[0], 4, 9, QRT, BLK)]
    got.append(gate(packed[4:6], [*got[0], share]))
    tab1, ltab1, *wides = call(
        functools.partial(other_tables_body, sz, spans),
        [extents, *halo, (tab2, VMEM), (ltab2, VMEM)],
        [(shape(*s), VMEM) for s in outs], [vm(2, ROW, BLK)], us=HINT,
    )
    tail = [(shape(2, 2, ROW, BLK), VMEM)] * 2
    out = None
    for k, count in enumerate(chunks):
        begin = begins[k]
        head, last = k == 0, k == len(chunks) - 1
        if k >= 1 and k + 2 < len(chunks):
            got.append(gate(packed[2 * k + 4 : 2 * k + 6], [*got[k], dtail]))
        ins = [extents, *((x, VMEM) for x in got[k]), *halo, (share, VMEM)]
        if k >= WIDE:
            ins += [(x, VMEM) for x in wides[2 * (k - WIDE) : 2 * (k - WIDE) + 2]]
        else:
            ins += [(x, VMEM) for x in (tab1, ltab1, tab2, ltab2)]
        outs = [(shape(2, beams, slots * BLK), HBM)]
        aliases = {}
        if not head:
            aliases[len(ins) + 2] = 0
            ins += [(dtail, VMEM), (ftail, VMEM), (out, HBM)]
        if not last:
            outs += tail
        low, top_slot = two_range(sz, begin, count)
        res = call(
            functools.partial(main_body, sz, begin, count, k >= WIDE), ins, outs,
            [vm(*d_s), vm(*f_s), vm(top_slot - low, 2, beams, BLK), DMA], aliases, us=HINT if head else 0.1,
        )
        out = res[0]
        if not last:
            dtail, ftail = res[1:]
    return out


def solution(mesh):
    placed = (
        P(None, None, ("strip", "sub")),
        P(("strip", "sub"), None, None, None, None),
        P(("strip", "sub"), None, None, None, None),
        P(("strip", "sub"), None, None, None, None),
        P("strip"),
    )
    return jax.shard_map(
        per_device,
        mesh=mesh,
        in_specs=placed,
        out_specs=P(None, None, ("strip", "sub")),
        check_vma=False,
    )
```
